128 devices in a mesh: prow: 4 (over x), pcol: 32 (over z, y, core).
Axes of the slice: x: 4, y: 4, z: 4, core: 2. Of those that a mesh axis runs over, the one named last changes fastest.
Arguments:
- trail_u: bfloat16 [8, 32, 2048, 256], P('prow', 'pcol'), may hold values from -6 to 6
- trail_v: bfloat16 [8, 32, 2048, 256], P('prow', 'pcol'), may hold values from -6 to 6
- tile_rank: int32 [8, 32], P('prow', 'pcol'), may hold values from 32 to 256
- new_rank: int32 [8, 32], P('prow', 'pcol'), may hold values from 32 to 256, as said below
- row_u: bfloat16 [8, 2048, 256], P('prow', 'pcol'), may hold values from -6 to 6
- row_v: bfloat16 [8, 2048, 256], P('prow', 'pcol'), may hold values from -0.23925781 to 0.23925781
- row_rank: int32 [8], replicated, may hold values from 32 to 256
- col_u: bfloat16 [32, 2048, 256], P('prow', 'pcol'), may hold values from -6 to 6
- col_v: bfloat16 [32, 2048, 256], P('prow', 'pcol'), may hold values from -0.23925781 to 0.23925781
- col_rank: int32 [32], replicated, may hold values from 32 to 256
- diag_inv: float32 [2048, 2048], P('pcol'), as said below
- sketch: bfloat16 [2048, 256], replicated, may hold values from -0.125 to 0.125
Outputs:
- fresh_u: bfloat16 [8, 32, 2048, 256], P('prow', 'pcol')
- fresh_v: bfloat16 [8, 32, 2048, 256], P('prow', 'pcol')
The draws below stay inside these ranges and needn't reach their ends.
Inputs may be any that keep to these rules, and one draw needn't show every extreme that they name: new_rank[i, j] is at most tile_rank[i, j]. `diag_inv`: lower triangular with diagonal entries between 1 and 2.
All inputs are finite; a program needn't handle non-finite values.
Results may differ from the reference program's by a relative error of at most 0.015.
Values may be sent and summed in bfloat16 or wider, within the bound.
No kernel may reach another device: no remote copies, remote signals or barrier semaphores. Data moves between devices by JAX's collectives and lax.ppermute only.
A program may use at most 128 MiB of HBM per device.

```python
import math
import jax
import jax.numpy as jnp
from jax import lax

B = 2048
RMAX = 256
TILE_ROWS = 8
TILE_COLS = 32


def shared_ranks(key):
    first, second, third, fourth = jax.random.split(key, 4)
    lowest = max(RMAX // 8, 1)
    count = TILE_ROWS * TILE_COLS
    ranks = jax.random.randint(first, (count,), lowest, RMAX + 1)
    place = jax.random.randint(second, (), 0, count)
    other = (place + 1 + jax.random.randint(third, (), 0, count - 1)) % count
    ranks = ranks.at[place].set(RMAX).at[other].set(lowest)
    share = jax.random.randint(fourth, (count,), 0, 1000)
    fresh = lowest + (ranks - lowest) * share // 999
    fresh = fresh.at[place].set(RMAX)
    return (ranks.reshape(TILE_ROWS, TILE_COLS).astype(jnp.int32), fresh.reshape(TILE_ROWS, TILE_COLS).astype(jnp.int32))


def draw_tile_rank(key, part):
    return shared_ranks(key)[0]


def draw_new_rank(key, part):
    return shared_ranks(key)[1]


def panel_ranks(key, count):
    first, second, third = jax.random.split(key, 3)
    lowest = max(RMAX // 8, 1)
    ranks = jax.random.randint(first, (count,), lowest, RMAX + 1)
    place = jax.random.randint(second, (), 0, count)
    other = (place + 1 + jax.random.randint(third, (), 0, count - 1)) % count
    return ranks.at[place].set(RMAX).at[other].set(lowest).astype(jnp.int32)


def draw_row_rank(key, part):
    key = jax.random.fold_in(key, 21)
    return panel_ranks(key, TILE_ROWS)


def draw_col_rank(key, part):
    key = jax.random.fold_in(key, 37)
    return panel_ranks(key, TILE_COLS)


def draw_diag_inv(key, part):
    key = jax.random.fold_in(key, 53)
    first, second = jax.random.split(key)
    spread = jax.random.normal(first, (B, B), jnp.float32) * (0.6 / B ** 0.5)
    main = jax.random.uniform(second, (B,), jnp.float32, 1.0, 2.0)
    places = jnp.arange(B)
    below = places[:, None] > places[None, :]
    return jnp.where(below, spread, 0.0) + jnp.diag(main)


def block_scale(rng, shape, pieces, least, top_value):
    def one(dim, shards_of):
        draws = jax.random.uniform(jax.random.fold_in(jax.random.fold_in(rng, 6), dim), (shards_of,), jnp.float32, least / len(pieces), top_value / len(pieces))
        return jnp.repeat(jnp.exp(draws), shape[dim] // shards_of).reshape((-1,) + (1,) * (len(shape) - dim - 1))

    level = one(*pieces[0])
    for cut in pieces[1:]:
        level = level * one(*cut)
    return level


def normal_values(rng, dims, deviation, most, cuts=(), kind=jnp.bfloat16):
    result = deviation * jax.random.normal(rng, dims, jnp.float32)
    if cuts:
        result = result * block_scale(rng, dims, cuts, -0.22, 0.18)
    return jnp.clip(result, -most, most).astype(kind)


def setup_inputs(seed: int = 0) -> dict:
    streams_of = jax.random.split(jax.random.key(seed), 13)
    trail_u = normal_values(streams_of[0], (TILE_ROWS, TILE_COLS, B, RMAX), 1.0, 6.0, ((0, 4), (1, 32)))
    trail_v = normal_values(streams_of[1], (TILE_ROWS, TILE_COLS, B, RMAX), 1.0, 6.0, ((0, 4), (1, 32)))
    tile_rank = draw_tile_rank(jax.random.fold_in(streams_of[12], 71), 0)
    new_rank = draw_new_rank(jax.random.fold_in(streams_of[12], 71), 0)
    row_u = normal_values(streams_of[4], (TILE_ROWS, B, RMAX), 1.0, 6.0, ((0, 4), (1, 32)))
    row_v = normal_values(streams_of[5], (TILE_ROWS, B, RMAX), 0.04, 0.23925781, ((0, 4), (1, 32)))
    row_rank = draw_row_rank(jax.random.fold_in(streams_of[12], 71), 0)
    col_u = normal_values(streams_of[7], (TILE_COLS, B, RMAX), 1.0, 6.0, ((0, 4), (1, 32)))
    col_v = normal_values(streams_of[8], (TILE_COLS, B, RMAX), 0.04, 0.23925781, ((0, 4), (1, 32)))
    col_rank = draw_col_rank(jax.random.fold_in(streams_of[12], 71), 0)
    diag_inv = draw_diag_inv(jax.random.fold_in(streams_of[12], 71), 0)
    sketch = normal_values(streams_of[11], (B, RMAX), B ** -0.5, 0.125)
    return {"trail_u": trail_u, "trail_v": trail_v, "tile_rank": tile_rank, "new_rank": new_rank, "row_u": row_u, "row_v": row_v, "row_rank": row_rank, "col_u": col_u, "col_v": col_v, "col_rank": col_rank, "diag_inv": diag_inv, "sketch": sketch}


def keep_columns(factor, rank):
    columns = jnp.arange(factor.shape[-1], dtype=jnp.int32)
    keep = (columns[None, :] < rank[:, None]).astype(factor.dtype)
    return factor * keep[:, None, :]

def solve_panel(diag_inv, right):

    def one_tile(tile):
        return jnp.dot(diag_inv, tile.astype(jnp.float32), precision=lax.Precision.HIGHEST).astype(jnp.bfloat16)
    return lax.map(one_tile, right)

def reference(trail_u, trail_v, tile_rank, new_rank, row_u, row_v, row_rank, col_u, col_v, col_rank, diag_inv, sketch):
    width = trail_u.shape[2]
    rmax = trail_u.shape[3]
    rows_u = keep_columns(row_u, row_rank)
    cols_u = keep_columns(col_u, col_rank)
    row_w = solve_panel(diag_inv, keep_columns(row_v, row_rank))
    col_w = solve_panel(diag_inv, keep_columns(col_v, col_rank))
    count = TILE_ROWS * TILE_COLS
    flat_index = jnp.arange(count, dtype=jnp.int32)
    row_index = flat_index // TILE_COLS
    col_index = flat_index % TILE_COLS
    columns = jnp.arange(rmax, dtype=jnp.int32)

    def one_tile(packed):
        left, right, rank_now, rank_new, i_row, j_col = packed
        alive = (columns < rank_now).astype(jnp.bfloat16)
        left = left * alive[None, :]
        right = right * alive[None, :]
        coupling = jnp.dot(row_w[i_row].T.astype(jnp.float32), col_w[j_col].astype(jnp.float32), preferred_element_type=jnp.float32).astype(jnp.bfloat16)
        shift = jnp.dot(cols_u[j_col].astype(jnp.float32), coupling.T.astype(jnp.float32), preferred_element_type=jnp.float32).astype(jnp.bfloat16)
        left_cat = jnp.concatenate([left, rows_u[i_row]], axis=1)
        right_cat = jnp.concatenate([right, -shift], axis=1)
        keep = columns < rank_new
        probe_in = sketch * keep.astype(jnp.bfloat16)[None, :]
        probe = jnp.dot(right_cat.T.astype(jnp.float32), probe_in.astype(jnp.float32), preferred_element_type=jnp.float32).astype(jnp.bfloat16)
        range_y = jnp.dot(left_cat.astype(jnp.float32), probe.astype(jnp.float32), preferred_element_type=jnp.float32)
        gram = jnp.dot(range_y.T, range_y, precision=lax.Precision.HIGHEST)
        gram = gram + jnp.diag(1.0 - keep.astype(jnp.float32))
        lower = jnp.linalg.cholesky(gram)
        basis = lax.linalg.triangular_solve(lower, range_y, left_side=False, lower=True, transpose_a=True)
        fresh_u = (basis * math.sqrt(width)).astype(jnp.bfloat16)
        back = jnp.dot(left_cat.T.astype(jnp.float32), fresh_u.astype(jnp.float32), preferred_element_type=jnp.float32).astype(jnp.bfloat16)
        fresh_v = (jnp.dot(right_cat.astype(jnp.float32), back.astype(jnp.float32), preferred_element_type=jnp.float32) / width).astype(jnp.bfloat16)
        return (fresh_u, fresh_v)
    fresh_u, fresh_v = lax.map(one_tile, (trail_u.reshape(count, width, rmax), trail_v.reshape(count, width, rmax), tile_rank.reshape(count), new_rank.reshape(count), row_index, col_index))
    return (fresh_u.reshape(TILE_ROWS, TILE_COLS, width, rmax), fresh_v.reshape(TILE_ROWS, TILE_COLS, width, rmax))
```

```python
import functools
import math

import jax
import jax.numpy as jnp
from jax import lax
from jax.experimental import pallas as pl
from jax.experimental.pallas import tpu as pltpu
from jax.sharding import Mesh, PartitionSpec as P

F32 = jnp.float32
BF16 = jnp.bfloat16
HALF = 128


def dot(a, b, ca=1, cb=0, precision=None):
    return lax.dot_general(
        a, b, (((ca,), (cb,)), ((), ())), preferred_element_type=F32, precision=precision
    )


def exact(a, b, ca=1, cb=0):
    return dot(a, b, ca, cb, lax.Precision.HIGHEST)


def pieces(x, count):
    out = []
    for _ in range(count):
        piece = x.astype(BF16)
        out.append(piece)
        x = x - piece.astype(F32)
    return out


def eliminate(blocks):
    n = HALF
    lane = lax.broadcasted_iota(jnp.int32, (8, n), 1)
    sub = lax.broadcasted_iota(jnp.int32, (8, n), 0)
    tiles = [[m[8 * i : 8 * i + 8] for i in range(n // 8)] for m in blocks]
    for k in range(0, n, 2):
        g, at = divmod(k, 8)
        first, second = lane == k, lane == k + 1
        pair = first | second
        for x in tiles:
            c0 = [jnp.broadcast_to(x[i][:, k : k + 1], (8, n)) for i in range(g, n // 8)]
            c1 = [jnp.broadcast_to(x[i][:, k + 1 : k + 2], (8, n)) for i in range(g, n // 8)]
            r0 = jnp.broadcast_to(x[g][at : at + 1], (8, n))
            r1 = jnp.broadcast_to(x[g][at + 1 : at + 2], (8, n))
            a = jnp.broadcast_to(c0[0][at : at + 1], (8, n))
            b = jnp.broadcast_to(c1[0][at : at + 1], (8, n))
            c = jnp.broadcast_to(c1[0][at + 1 : at + 2], (8, n))
            inv = 1.0 / (a * c - b * b)
            ai, bi, ci = a * inv, b * inv, c * inv
            r0 = jnp.where(first, 1.0, jnp.where(second, 0.0, r0))
            r1 = jnp.where(second, 1.0, jnp.where(first, 0.0, r1))
            q0 = ci * r0 - bi * r1
            q1 = ai * r1 - bi * r0
            for m, i in enumerate(range(g, n // 8)):
                if i == g and at == 6:
                    continue
                new = (jnp.where(pair, 0.0, x[i]) - c0[m] * q0) - c1[m] * q1
                x[i] = jnp.where(sub > at + 1, new, x[i]) if i == g else new
    odd = (sub % 2) == 1
    out = []
    for x in tiles:
        done = []
        for i in range(n // 8):
            row = sub + 8 * i
            pivot_start = row - row % 2
            here = jnp.sum(jnp.where(lane == row, x[i], 0.0), axis=1, keepdims=True)
            above = jnp.sum(jnp.where((lane == row + 1) & ~odd, x[i], 0.0), axis=1, keepdims=True)
            here = jnp.broadcast_to(here, (8, n))
            above = jnp.broadcast_to(above, (8, n))
            unit = jnp.where(lane < pivot_start, x[i], jnp.where(lane == row, 1.0, 0.0))
            ratio = jnp.where(odd, pltpu.roll(above / here, 1, axis=0), 0.0)
            above = jnp.where(odd, pltpu.roll(above, 1, axis=0), 0.0)
            scale = lax.rsqrt(here - ratio * above)
            done.append((unit - ratio * pltpu.roll(unit, 1, axis=0)) * scale)
        out.append(jnp.concatenate(done, axis=0))
    return out


def inverse_factors(grams):
    h = HALF
    m1 = eliminate([g[:h, :h] for g in grams])
    u12 = [exact(m, g[:h, h:]) for m, g in zip(m1, grams)]
    m2 = eliminate([g[h:, h:] - exact(u, u, 0, 0) for u, g in zip(u12, grams)])
    m21 = [-exact(b, exact(u, a, 0, 0)) for a, b, u in zip(m1, m2, u12)]
    zero = jnp.zeros((h, h), F32)
    return [
        jnp.concatenate(
            [jnp.concatenate([a, zero], axis=1), jnp.concatenate([c, b], axis=1)], axis=0
        )
        for a, b, c in zip(m1, m2, m21)
    ]


def tail_kernel(
    ranks,
    guu,
    pt,
    sk,
    gathered,
    vp0,
    vp1,
    vp2,
    vp3,
    up0,
    up1,
    up2,
    up3,
    trail_u,
    trail_v,
    fresh_u,
    fresh_v,
    dinv,
    vall,
    ui,
    uj,
    tu,
    tv,
    zs,
    bs,
    ou,
    ov,
    load_sem,
    out_sem,
):
    width, rmax = 2048, 256
    part = width // 4
    here = ranks[7]

    loads = []

    def load(src, dst):
        copy = pltpu.make_async_copy(src, dst, load_sem.at[len(loads)])
        copy.start()
        loads.append(copy)
        return copy

    need_v = [load(gathered.at[8 + t], vall.at[:, pl.ds(rmax * t, rmax)]) for t in range(2)]
    for k, src in enumerate((vp0, vp1, vp2, vp3)):
        at = pl.multiple_of(lax.rem(here + 4 - k, 4) * part, part)
        need_v.append(load(src, vall.at[pl.ds(at, part), pl.ds(2 * rmax, rmax)]))
    need_d = []
    for q in range(4):
        chunks, rows = pl.ds(0, 2 * q + 2), pl.ds(part * q, part)
        need_d.append(load(gathered.at[chunks, rows], dinv.at[chunks, rows]))
    need_u = [load(gathered.at[10 + t], ui.at[t]) for t in range(2)]
    need_u.append(load(trail_u, tu))
    need_uj = []
    for k, src in enumerate((up0, up1, up2, up3)):
        at = pl.multiple_of(lax.rem(here + 4 - k, 4) * part, part)
        need_uj.append(load(src, uj.at[pl.ds(at, part)]))
    need_tv = load(trail_v, tv)

    for copy in need_v:
        copy.wait()
    coupling = [jnp.zeros((rmax, rmax), F32)] * 2
    for q in range(4):
        need_d[q].wait()
        depth = part * (q + 1)
        for n in range(2):
            at = part * q + rmax * n
            lhs = jnp.concatenate([dinv[c, at : at + rmax] for c in range(2 * q + 2)], axis=1)
            w = dot(lhs, vall[:depth]).astype(BF16)
            wj = w[:, 2 * rmax :]
            coupling = [
                coupling[t] + dot(w[:, rmax * t : rmax * (t + 1)], wj, 0, 0) for t in range(2)
            ]
    for copy in need_u:
        copy.wait()
    gur = [dot(tu[t], ui[t], 0, 0) for t in range(2)]
    grr = [dot(ui[t], ui[t], 0, 0) for t in range(2)]
    for copy in need_uj:
        copy.wait()
    reach = dot(uj[...], sk[...], 0, 0).astype(BF16)

    row = lax.broadcasted_iota(jnp.int32, (rmax, rmax), 0)
    col = lax.broadcasted_iota(jnp.int32, (rmax, rmax), 1)
    couplings, grams, probes, whole, heads = [], [], [], [], []
    for t in range(2):
        tile_rank, new_rank, row_rank, col_rank = ranks[t], ranks[2 + t], ranks[4 + t], ranks[6]
        keep = col < new_rank
        c = jnp.where((row < row_rank) & (col < col_rank), coupling[t], 0.0).astype(BF16)
        top = jnp.where((row < tile_rank) & keep, pt[t], 0.0)
        bottom = jnp.where(keep, -dot(c, reach), 0.0)
        probe = jnp.concatenate([top, bottom], axis=0).astype(BF16)
        g = jnp.concatenate(
            [
                jnp.concatenate([guu[t], gur[t]], axis=1),
                jnp.concatenate([gur[t].T, grr[t]], axis=1),
            ],
            axis=0,
        )
        parts = pieces(g, 3)
        gp = dot(parts[0], probe) + (dot(parts[1], probe) + dot(parts[2], probe))
        gp = pieces(gp, 3)
        gram = dot(probe, gp[0], 0, 0) + (dot(probe, gp[1], 0, 0) + dot(probe, gp[2], 0, 0))
        grams.append(gram + jnp.where((row == col) & ~keep, 1.0, 0.0))
        couplings.append(c)
        probes.append(probe)
        whole.append(parts)
    inverses = inverse_factors(grams)
    need_tv.wait()
    for t in range(2):
        mp = pieces(inverses[t] * math.sqrt(width), 3)
        z = dot(probes[t], mp[0], 1, 1) + (dot(probes[t], mp[1], 1, 1) + dot(probes[t], mp[2], 1, 1))
        z = z.astype(BF16)
        back = dot(whole[t][0], z) + dot(whole[t][1], z)
        top = jnp.where(row < ranks[t], back[:rmax], 0.0)
        bottom = -dot(couplings[t], back[rmax:].astype(BF16), 0, 0)
        zs[t] = z
        bs[t] = (jnp.concatenate([top, bottom], axis=0) / width).astype(BF16)

    copies = []
    for t in range(2):
        for n in range(4):
            rows = pl.ds(part * n, part)
            left = jnp.concatenate([tu[t, rows], ui[t, rows]], axis=1)
            ou[t, rows] = dot(left, zs[t]).astype(BF16)
            right = jnp.concatenate([tv[t, rows], uj[rows]], axis=1)
            ov[t, rows] = dot(right, bs[t]).astype(BF16)
            for src, dst in ((ou, fresh_u), (ov, fresh_v)):
                copy = pltpu.make_async_copy(
                    src.at[t, rows], dst.at[t, rows], out_sem.at[len(copies)]
                )
                copy.start()
                copies.append(copy)
    for copy in copies:
        copy.wait()


def tail(ranks, guu, pt, sketch, gathered, vparts, uparts, trail_u, trail_v):
    width, rmax = sketch.shape
    vmem = pl.BlockSpec(memory_space=pltpu.VMEM)
    hbm = pl.BlockSpec(memory_space=pl.ANY)
    tile = jax.ShapeDtypeStruct(trail_u.shape, BF16)
    return pl.pallas_call(
        tail_kernel,
        name="tail",
        out_shape=(tile, tile),
        in_specs=[pl.BlockSpec(memory_space=pltpu.SMEM)] + [vmem] * 3 + [hbm] * 11,
        out_specs=(hbm, hbm),
        scratch_shapes=[
            pltpu.VMEM((8, width, rmax), BF16),
            pltpu.VMEM((width, 3 * rmax), BF16),
            pltpu.VMEM((2, width, rmax), BF16),
            pltpu.VMEM((width, rmax), BF16),
            pltpu.VMEM((2, width, rmax), BF16),
            pltpu.VMEM((2, width, rmax), BF16),
            pltpu.VMEM((2, 2 * rmax, rmax), BF16),
            pltpu.VMEM((2, 2 * rmax, rmax), BF16),
            pltpu.VMEM((2, width, rmax), BF16),
            pltpu.VMEM((2, width, rmax), BF16),
            pltpu.SemaphoreType.DMA((20,)),
            pltpu.SemaphoreType.DMA((16,)),
        ],
        compiler_params=pltpu.CompilerParams(vmem_limit_bytes=56 * 1024 * 1024),
        cost_estimate=pl.CostEstimate(
            flops=16_000_000_000, bytes_accessed=20_000_000, transcendentals=0
        ),
    )(ranks, guu, pt, sketch, gathered, *vparts, *uparts, trail_u, trail_v)


def on_device(
    trail_u,
    trail_v,
    tile_rank,
    new_rank,
    row_u,
    row_v,
    row_rank,
    col_u,
    col_v,
    col_rank,
    diag_inv,
    sketch,
):
    trow, _, width, rmax = trail_u.shape
    x, z = lax.axis_index("x"), lax.axis_index("z")
    yc = lax.axis_index(("y", "c"))
    pcol = z * 8 + yc
    trail_u, trail_v = trail_u[:, 0], trail_v[:, 0]

    slab = diag_inv.shape[0]
    factor = jnp.swapaxes(diag_inv.astype(BF16).reshape(slab, width // rmax, rmax), 0, 1)
    mine = jnp.concatenate([factor, row_v, row_u], axis=0)
    gathered = lax.all_gather(mine, ("z", "y", "c"), axis=1, tiled=True)

    both = jnp.stack([col_v, col_u], axis=1)
    quarter = lax.all_to_all(both, ("y", "c"), split_axis=0, concat_axis=2, tiled=True)[0]
    swap = [(a * 4 + b, b * 4 + a) for a in range(4) for b in range(4)]
    quarter = lax.ppermute(quarter, ("x", "z"), swap)

    def spread(block):
        return [block] + [
            lax.ppermute(block, "x", [(a, (a + k) % 4) for a in range(4)]) for k in (1, 3, 2)
        ]

    vparts = spread(quarter[0])
    uparts = spread(quarter[1])
    vparts = [vparts[0], vparts[1], vparts[3], vparts[2]]
    uparts = [uparts[0], uparts[1], uparts[3], uparts[2]]

    guu = jnp.einsum("tbm,tbn->tmn", trail_u, trail_u, preferred_element_type=F32)
    pt = jnp.einsum("tbm,bn->tmn", trail_v, sketch, preferred_element_type=F32)
    own_row = lax.dynamic_slice_in_dim(row_rank, x * trow, trow)
    own_col = lax.dynamic_slice_in_dim(col_rank, pcol, 1)
    ranks = jnp.concatenate([tile_rank[:, 0], new_rank[:, 0], own_row, own_col, x[None]])
    fresh_u, fresh_v = tail(ranks, guu, pt, sketch, gathered, vparts, uparts, trail_u, trail_v)
    return fresh_u[:, None], fresh_v[:, None]


def solution(mesh):
    split = Mesh(mesh.devices.reshape(4, 4, 4, 2), ("x", "z", "y", "c"))
    cols = ("z", "y", "c")
    tiles = P("x", cols, None, None)
    panel = P("x", cols, None)
    return jax.shard_map(
        on_device,
        mesh=split,
        in_specs=(
            tiles,
            tiles,
            P("x", cols),
            P("x", cols),
            panel,
            panel,
            P(),
            panel,
            panel,
            P(),
            P(cols, None),
            P(),
        ),
        out_specs=(tiles, tiles),
        check_vma=False,
    )
```

```python
import functools
import math

import jax
import jax.numpy as jnp
from jax import lax
from jax.experimental import pallas as pl
from jax.experimental.pallas import tpu as pltpu
from jax.sharding import Mesh, PartitionSpec as P

F32 = jnp.float32
BF16 = jnp.bfloat16
HALF = 128


def dot(a, b, ca=1, cb=0, precision=None):
    return lax.dot_general(
        a, b, (((ca,), (cb,)), ((), ())), preferred_element_type=F32, precision=precision
    )


def exact(a, b, ca=1, cb=0):
    return dot(a, b, ca, cb, lax.Precision.HIGHEST)


def pieces(x, count):
    out = []
    for _ in range(count):
        piece = x.astype(BF16)
        out.append(piece)
        x = x - piece.astype(F32)
    return out


def reciprocal(x):
    r = pl.reciprocal(x, approx=True)
    return r * (2.0 - x * r)

def tree(terms):
    while len(terms) > 1:
        terms = [a + b for a, b in zip(terms[::2], terms[1::2])] + (terms[-1:] if len(terms) % 2 else [])
    return terms[0]

def eliminate(blocks):
    n = HALF
    groups = n // 8
    lane = lax.broadcasted_iota(jnp.int32, (8, n), 1)
    sub = lax.broadcasted_iota(jnp.int32, (8, n), 0)
    spread = lambda v, r: jnp.broadcast_to(v[r : r + 1], (8, n))
    tiles = [[m[8 * i : 8 * i + 8] for i in range(groups)] for m in blocks]
    for g in range(groups):
        panel = (lane >= 8 * g) & (lane < 8 * g + 8)
        for x in tiles:
            cols = [[jnp.broadcast_to(x[i][:, 8 * g + j : 8 * g + j + 1], (8, n)) for i in range(g, groups)] for j in range(8)]
            top = x[g]
            factors = []
            for m in range(0, 8, 2):
                c0, c1 = cols[m], cols[m + 1]
                a, b, c = spread(c0[0], m), spread(c1[0], m), spread(c1[0], m + 1)
                inv = reciprocal(a * c - b * b)
                ai, bi, ci = a * inv, b * inv, c * inv
                for j in range(m + 2, 8):
                    s0, s1 = spread(c0[0], j), spread(c1[0], j)
                    g0, g1 = ci * s0 - bi * s1, ai * s1 - bi * s0
                    cols[j] = [v - (p * g0 + q * g1) for v, p, q in zip(cols[j], c0, c1)]
                k = 8 * g + m
                later = (lane > k + 1) & (lane < 8 * g + 8)
                r0, r1 = spread(top, m), spread(top, m + 1)
                first, second = lane == k, lane == k + 1
                r0 = jnp.where(first, 1.0, jnp.where(second, 0.0, r0))
                r1 = jnp.where(second, 1.0, jnp.where(first, 0.0, r1))
                q0, q1 = ci * r0 - bi * r1, ai * r1 - bi * r0
                if m < 6:
                    new = jnp.where(first | second, 0.0, top) - (c0[0] * q0 + c1[0] * q1)
                    top = jnp.where(sub > m + 1, new, top)
                factors.append((jnp.where(later, 0.0, q0), jnp.where(later, 0.0, q1)))
            x[g] = top
            for t in range(1, groups - g):
                terms = [cols[2 * p][t] * q0 + cols[2 * p + 1][t] * q1 for p, (q0, q1) in enumerate(factors)]
                x[g + t] = jnp.where(panel, 0.0, x[g + t]) - tree(terms)
    odd = (sub % 2) == 1
    out = []
    for x in tiles:
        done = []
        for i in range(groups):
            row = sub + 8 * i
            pivot_start = row - row % 2
            here = jnp.sum(jnp.where(lane == row, x[i], 0.0), axis=1, keepdims=True)
            above = jnp.sum(jnp.where((lane == row + 1) & ~odd, x[i], 0.0), axis=1, keepdims=True)
            here = jnp.broadcast_to(here, (8, n))
            above = jnp.broadcast_to(above, (8, n))
            unit = jnp.where(lane < pivot_start, x[i], jnp.where(lane == row, 1.0, 0.0))
            ratio = jnp.where(odd, pltpu.roll(above / here, 1, axis=0), 0.0)
            above = jnp.where(odd, pltpu.roll(above, 1, axis=0), 0.0)
            scale = lax.rsqrt(here - ratio * above)
            done.append((unit - ratio * pltpu.roll(unit, 1, axis=0)) * scale)
        out.append(jnp.concatenate(done, axis=0))
    return out


def inverse_factors(grams):
    h = HALF
    m1 = eliminate([g[:h, :h] for g in grams])
    u12 = [exact(m, g[:h, h:]) for m, g in zip(m1, grams)]
    m2 = eliminate([g[h:, h:] - exact(u, u, 0, 0) for u, g in zip(u12, grams)])
    m21 = [-exact(b, exact(u, a, 0, 0)) for a, b, u in zip(m1, m2, u12)]
    zero = jnp.zeros((h, h), F32)
    return [
        jnp.concatenate(
            [jnp.concatenate([a, zero], axis=1), jnp.concatenate([c, b], axis=1)], axis=0
        )
        for a, b, c in zip(m1, m2, m21)
    ]


def prepare_kernel(ranks, tu, tv, sk, probe, upper, gram):
    rmax = sk.shape[1]
    t = pl.program_id(0)
    row = lax.broadcasted_iota(jnp.int32, (rmax, rmax), 0)
    col = lax.broadcasted_iota(jnp.int32, (rmax, rmax), 1)
    p = dot(tv[0], sk[...], 0, 0)
    p = jnp.where((row < ranks[t]) & (col < ranks[2 + t]), p, 0.0).astype(BF16)
    h = sum(dot(piece, p) for piece in pieces(dot(tu[0], tu[0], 0, 0), 3))
    probe[0] = p
    upper[0] = h
    gram[0] = 0.5 * sum(dot(p, piece, 0, 0) for piece in pieces(h, 3))


def prepare(ranks, trail_u, trail_v, sketch):
    width, rmax = sketch.shape
    square = lambda kind: jax.ShapeDtypeStruct((2, rmax, rmax), kind)
    tile = pl.BlockSpec((1, width, rmax), lambda t: (t, 0, 0))
    small = pl.BlockSpec((1, rmax, rmax), lambda t: (t, 0, 0))
    return pl.pallas_call(
        prepare_kernel,
        name="prepare",
        grid=(2,),
        out_shape=(square(BF16), square(F32), square(F32)),
        in_specs=[
            pl.BlockSpec(memory_space=pltpu.SMEM),
            tile,
            tile,
            pl.BlockSpec((width, rmax), lambda t: (0, 0)),
        ],
        out_specs=(small, small, small),
        compiler_params=pltpu.CompilerParams(vmem_limit_bytes=24 * 1024 * 1024),
        cost_estimate=pl.CostEstimate(
            flops=2_000_000_000, bytes_accessed=6_000_000, transcendentals=0
        ),
    )(ranks, trail_u, trail_v, sketch)


def reach_kernel(ranks, sk, up0, up1, up2, up3, out):
    part = up0.shape[0]
    total = None
    for k, block in enumerate((up0, up1, up2, up3)):
        at = pl.multiple_of(ranks[7 + k] * part, part)
        term = dot(block[...], sk[pl.ds(at, part)], 0, 0)
        total = term if total is None else total + term
    out[...] = total.astype(BF16)


def reach_of(ranks, sketch, uparts):
    rmax = sketch.shape[1]
    vmem = pl.BlockSpec(memory_space=pltpu.VMEM)
    return pl.pallas_call(
        reach_kernel,
        name="reach",
        out_shape=jax.ShapeDtypeStruct((rmax, rmax), BF16),
        in_specs=[pl.BlockSpec(memory_space=pltpu.SMEM)] + [vmem] * 5,
        out_specs=vmem,
        compiler_params=pltpu.CompilerParams(vmem_limit_bytes=12 * 1024 * 1024),
        cost_estimate=pl.CostEstimate(
            flops=300_000_000, bytes_accessed=2_200_000, transcendentals=0
        ),
    )(ranks, sketch, *uparts)


def tail_kernel(
    ranks,
    probe,
    upper,
    half,
    reach,
    gathered,
    vp0,
    vp1,
    vp2,
    vp3,
    up0,
    up1,
    up2,
    up3,
    trail_u,
    trail_v,
    fresh_u,
    fresh_v,
    dinv,
    vall,
    ui,
    uj,
    tu,
    tv,
    zs,
    bs,
    ou,
    ov,
    load_sem,
    out_sem,
):
    width, rmax = uj.shape
    part = width // 4
    loads = []

    def load(src, dst):
        copy = pltpu.make_async_copy(src, dst, load_sem.at[len(loads)])
        copy.start()
        loads.append(copy)
        return copy

    def spots():
        return [pl.multiple_of(ranks[7 + k] * part, part) for k in range(4)]

    need_v = [load(gathered.at[8 + t], vall.at[:, pl.ds(rmax * t, rmax)]) for t in range(2)]
    for at, src in zip(spots(), (vp0, vp1, vp2, vp3)):
        need_v.append(load(src, vall.at[pl.ds(at, part), pl.ds(2 * rmax, rmax)]))
    need_d = []
    for q in range(4):
        chunks, rows = pl.ds(0, 2 * q + 2), pl.ds(part * q, part)
        need_d.append(load(gathered.at[chunks, rows], dinv.at[chunks, rows]))
    need_u = [load(gathered.at[10 + t], ui.at[t]) for t in range(2)]
    need_u.append(load(trail_u, tu))
    rest = [load(src, uj.at[pl.ds(at, part)]) for at, src in zip(spots(), (up0, up1, up2, up3))]
    rest.append(load(trail_v, tv))

    for copy in need_v:
        copy.wait()
    coupling = [jnp.zeros((rmax, rmax), F32)] * 2
    for q in range(4):
        need_d[q].wait()
        for n in range(2):
            at = part * q + rmax * n
            count = 2 * q + 1 + n
            lhs = jnp.concatenate([dinv[c, at : at + rmax] for c in range(count)], axis=1)
            w = dot(lhs, vall[: rmax * count]).astype(BF16)
            wj = w[:, 2 * rmax :]
            coupling = [
                coupling[t] + dot(w[:, rmax * t : rmax * (t + 1)], wj, 0, 0) for t in range(2)
            ]
    for copy in need_u:
        copy.wait()

    row = lax.broadcasted_iota(jnp.int32, (rmax, rmax), 0)
    col = lax.broadcasted_iota(jnp.int32, (rmax, rmax), 1)
    couplings, grams, probes, products = [], [], [], []
    for t in range(2):
        new_rank, row_rank, col_rank = ranks[2 + t], ranks[4 + t], ranks[6]
        keep = col < new_rank
        top = probe[t]
        c = jnp.where((row < row_rank) & (col < col_rank), coupling[t], 0.0).astype(BF16)
        bottom = jnp.where(keep, -dot(c, reach[...]), 0.0).astype(BF16)
        gur = pieces(dot(tu[t], ui[t], 0, 0), 3)
        grr = pieces(dot(ui[t], ui[t], 0, 0), 3)
        cross = sum(dot(piece, top, 0, 0) for piece in gur)
        own = sum(dot(piece, bottom) for piece in grr)
        mixed = pieces(cross + 0.5 * own, 3)
        gram = half[t] + sum(dot(bottom, piece, 0, 0) for piece in mixed)
        grams.append(gram + gram.T + jnp.where((row == col) & ~keep, 1.0, 0.0))
        couplings.append(c)
        probes.append(jnp.concatenate([top, bottom], axis=0))
        above = upper[t] + sum(dot(piece, bottom) for piece in gur[:2])
        products.append(pieces(jnp.concatenate([above, cross + own], axis=0), 2))
    inverses = inverse_factors(grams)
    for t in range(2):
        m = pieces(inverses[t] * math.sqrt(width), 2)
        zs[t] = (dot(probes[t], m[0], 1, 1) + dot(probes[t], m[1], 1, 1)).astype(BF16)
        g = products[t]
        back = dot(g[0], m[0], 1, 1) + (dot(g[0], m[1], 1, 1) + dot(g[1], m[0], 1, 1))
        top = jnp.where(row < ranks[t], back[:rmax], 0.0)
        bottom = -dot(couplings[t], back[rmax:].astype(BF16), 0, 0)
        bs[t] = (jnp.concatenate([top, bottom], axis=0) / width).astype(BF16)
    for copy in rest:
        copy.wait()

    copies = []
    for t in range(2):
        for n in range(4):
            rows = pl.ds(part * n, part)
            left = jnp.concatenate([tu[t, rows], ui[t, rows]], axis=1)
            ou[t, rows] = dot(left, zs[t]).astype(BF16)
            right = jnp.concatenate([tv[t, rows], uj[rows]], axis=1)
            ov[t, rows] = dot(right, bs[t]).astype(BF16)
            for src, dst in ((ou, fresh_u), (ov, fresh_v)):
                copy = pltpu.make_async_copy(
                    src.at[t, rows], dst.at[t, rows], out_sem.at[len(copies)]
                )
                copy.start()
                copies.append(copy)
    for copy in copies:
        copy.wait()


def tail(ranks, probe, upper, half, reach, gathered, vparts, uparts, trail_u, trail_v):
    _, width, rmax = trail_u.shape
    vmem = pl.BlockSpec(memory_space=pltpu.VMEM)
    hbm = pl.BlockSpec(memory_space=pl.ANY)
    tile = jax.ShapeDtypeStruct(trail_u.shape, BF16)
    return pl.pallas_call(
        tail_kernel,
        name="tail",
        out_shape=(tile, tile),
        in_specs=[pl.BlockSpec(memory_space=pltpu.SMEM)] + [vmem] * 4 + [hbm] * 11,
        out_specs=(hbm, hbm),
        scratch_shapes=[
            pltpu.VMEM((8, width, rmax), BF16),
            pltpu.VMEM((width, 3 * rmax), BF16),
            pltpu.VMEM((2, width, rmax), BF16),
            pltpu.VMEM((width, rmax), BF16),
            pltpu.VMEM((2, width, rmax), BF16),
            pltpu.VMEM((2, width, rmax), BF16),
            pltpu.VMEM((2, 2 * rmax, rmax), BF16),
            pltpu.VMEM((2, 2 * rmax, rmax), BF16),
            pltpu.VMEM((2, width, rmax), BF16),
            pltpu.VMEM((2, width, rmax), BF16),
            pltpu.SemaphoreType.DMA((18,)),
            pltpu.SemaphoreType.DMA((16,)),
        ],
        compiler_params=pltpu.CompilerParams(vmem_limit_bytes=44 * 1024 * 1024),
        cost_estimate=pl.CostEstimate(
            flops=16_000_000_000, bytes_accessed=20_000_000, transcendentals=0
        ),
    )(ranks, probe, upper, half, reach, gathered, *vparts, *uparts, trail_u, trail_v)


def on_device(
    trail_u,
    trail_v,
    tile_rank,
    new_rank,
    row_u,
    row_v,
    row_rank,
    col_u,
    col_v,
    col_rank,
    diag_inv,
    sketch,
):
    trow, _, width, rmax = trail_u.shape
    x, z = lax.axis_index("x"), lax.axis_index("z")
    yc = lax.axis_index(("y", "c"))
    pcol = z * 8 + yc
    trail_u, trail_v = trail_u[:, 0], trail_v[:, 0]

    slab = diag_inv.shape[0]
    factor = jnp.swapaxes(diag_inv.astype(BF16).reshape(slab, width // rmax, rmax), 0, 1)
    mine = jnp.concatenate([factor, row_v, row_u], axis=0)
    gathered = lax.all_gather(mine, ("z", "y", "c"), axis=1, tiled=True)

    both = jnp.stack([col_v, col_u], axis=1)
    quarter = lax.all_to_all(both, ("y", "c"), split_axis=0, concat_axis=2, tiled=True)[0]
    times = (0, 2, 3, 1)
    swap = [(a * 4 + q, (times[a] ^ q) * 4 + a) for a in range(4) for q in range(4)]
    quarter = lax.ppermute(quarter, ("x", "z"), swap)

    def spread(block):
        return [block] + [
            lax.ppermute(block, "x", [(a, (a + k) % 4) for a in range(4)]) for k in (1, 3, 2)
        ]

    vparts = spread(quarter[0])
    uparts = spread(quarter[1])
    vparts = [vparts[0], vparts[1], vparts[3], vparts[2]]
    uparts = [uparts[0], uparts[1], uparts[3], uparts[2]]

    own_row = lax.dynamic_slice_in_dim(row_rank, x * trow, trow)
    own_col = lax.dynamic_slice_in_dim(col_rank, pcol, 1)
    turn = jnp.array(times, jnp.int32)[z]
    quarters = [(turn ^ lax.rem(x + 4 - k, 4))[None] for k in range(4)]
    ranks = jnp.concatenate([tile_rank[:, 0], new_rank[:, 0], own_row, own_col] + quarters)
    probe, upper, half = prepare(ranks, trail_u, trail_v, sketch)
    reach = reach_of(ranks, sketch, uparts)
    fresh_u, fresh_v = tail(
        ranks, probe, upper, half, reach, gathered, vparts, uparts, trail_u, trail_v
    )
    return fresh_u[:, None], fresh_v[:, None]


def solution(mesh):
    split = Mesh(mesh.devices.reshape(4, 4, 4, 2), ("x", "z", "y", "c"))
    cols = ("z", "y", "c")
    tiles = P("x", cols, None, None)
    panel = P("x", cols, None)
    return jax.shard_map(
        on_device,
        mesh=split,
        in_specs=(
            tiles,
            tiles,
            P("x", cols),
            P("x", cols),
            panel,
            panel,
            P(),
            panel,
            panel,
            P(),
            P(cols, None),
            P(),
        ),
        out_specs=(tiles, tiles),
        check_vma=False,
    )
```

```python
import functools
import math

import jax
import jax.numpy as jnp
from jax import lax
from jax.experimental import pallas as pl
from jax.experimental.pallas import tpu as pltpu
from jax.sharding import Mesh, PartitionSpec as P

F32 = jnp.float32
BF16 = jnp.bfloat16
HALF = 128


def dot(a, b, ca=1, cb=0, precision=None):
    return lax.dot_general(
        a, b, (((ca,), (cb,)), ((), ())), preferred_element_type=F32, precision=precision
    )


def exact(a, b, ca=1, cb=0):
    return dot(a, b, ca, cb, lax.Precision.HIGHEST)


def pieces(x, count):
    out = []
    for _ in range(count):
        piece = x.astype(BF16)
        out.append(piece)
        x = x - piece.astype(F32)
    return out


def reciprocal(x):
    r = pl.reciprocal(x, approx=True)
    return r * (2.0 - x * r)

def tree(terms):
    while len(terms) > 1:
        terms = [a + b for a, b in zip(terms[::2], terms[1::2])] + (terms[-1:] if len(terms) % 2 else [])
    return terms[0]

def eliminate(blocks):
    n = HALF
    groups = n // 8
    lane = lax.broadcasted_iota(jnp.int32, (8, n), 1)
    sub = lax.broadcasted_iota(jnp.int32, (8, n), 0)
    spread = lambda v, r: jnp.broadcast_to(v[r : r + 1], (8, n))
    tiles = [[m[8 * i : 8 * i + 8] for i in range(groups)] for m in blocks]

    def column(v, at):
        return jnp.broadcast_to(jnp.sum(jnp.where(lane == at, v, 0.0), axis=1, keepdims=True), (8, n))

    for g in range(groups):
        panel = (lane >= 8 * g) & (lane < 8 * g + 8)
        for x in tiles:
            cols = [[column(x[i], 8 * g + j) for j in range(8)] for i in range(g, groups)]
            top, own, kept = x[g], cols[0], x[g]
            for m in range(0, 8, 2):
                c0, c1 = own[m], own[m + 1]
                a, b, c = spread(c0, m), spread(c1, m), spread(c1, m + 1)
                inv = reciprocal(a * c - b * b)
                ai, bi, ci = a * inv, b * inv, c * inv
                upper, lower = sub == m, sub == m + 1
                for j in range(m + 2, 8):
                    s0, s1 = spread(own[j], m), spread(own[j], m + 1)
                    g0, g1 = ci * s0 - bi * s1, ai * s1 - bi * s0
                    own[j] = jnp.where(upper, g0, jnp.where(lower, g1, own[j] - (c0 * g0 + c1 * g1)))
                k = 8 * g + m
                first, second = lane == k, lane == k + 1
                if m:
                    kept = jnp.where(upper | lower, top, kept)
                r0, r1 = spread(top, m), spread(top, m + 1)
                r0 = jnp.where(first, 1.0, jnp.where(second, 0.0, r0))
                r1 = jnp.where(second, 1.0, jnp.where(first, 0.0, r1))
                q0, q1 = ci * r0 - bi * r1, ai * r1 - bi * r0
                new = jnp.where(first | second, 0.0, top) - (c0 * q0 + c1 * q1)
                top = jnp.where(upper, q0, jnp.where(lower, q1, new))
            x[g] = kept
            if g + 1 < groups:
                solved = [spread(top, m) for m in range(8)]
                for t in range(1, groups - g):
                    terms = [cols[t][m] * solved[m] for m in range(8)]
                    x[g + t] = jnp.where(panel, 0.0, x[g + t]) - tree(terms)
    odd = (sub % 2) == 1
    out = []
    for x in tiles:
        done = []
        for i in range(groups):
            row = sub + 8 * i
            pivot_start = row - row % 2
            here = jnp.sum(jnp.where(lane == row, x[i], 0.0), axis=1, keepdims=True)
            above = jnp.sum(jnp.where((lane == row + 1) & ~odd, x[i], 0.0), axis=1, keepdims=True)
            here = jnp.broadcast_to(here, (8, n))
            above = jnp.broadcast_to(above, (8, n))
            unit = jnp.where(lane < pivot_start, x[i], jnp.where(lane == row, 1.0, 0.0))
            ratio = jnp.where(odd, pltpu.roll(above / here, 1, axis=0), 0.0)
            above = jnp.where(odd, pltpu.roll(above, 1, axis=0), 0.0)
            scale = lax.rsqrt(here - ratio * above)
            done.append((unit - ratio * pltpu.roll(unit, 1, axis=0)) * scale)
        out.append(jnp.concatenate(done, axis=0))
    return out


def inverse_factors(grams):
    h = HALF
    m1 = eliminate([g[:h, :h] for g in grams])
    u12 = [exact(m, g[:h, h:]) for m, g in zip(m1, grams)]
    m2 = eliminate([g[h:, h:] - exact(u, u, 0, 0) for u, g in zip(u12, grams)])
    m21 = [-exact(b, exact(u, a, 0, 0)) for a, b, u in zip(m1, m2, u12)]
    zero = jnp.zeros((h, h), F32)
    return [
        jnp.concatenate(
            [jnp.concatenate([a, zero], axis=1), jnp.concatenate([c, b], axis=1)], axis=0
        )
        for a, b, c in zip(m1, m2, m21)
    ]


def pack_kernel(diag, row_v, row_u, out):
    chunks = out.shape[0] - 4
    rmax = out.shape[2]
    for c in range(chunks):
        out[c] = diag[:, rmax * c : rmax * (c + 1)].astype(BF16)
    out[chunks : chunks + 2] = row_v[...]
    out[chunks + 2 :] = row_u[...]


def pack(diag_inv, row_v, row_u):
    count, slab, rmax = row_v.shape
    chunks = diag_inv.shape[1] // rmax
    return pl.pallas_call(
        pack_kernel,
        name="pack",
        out_shape=jax.ShapeDtypeStruct((chunks + 2 * count, slab, rmax), BF16),
        cost_estimate=pl.CostEstimate(flops=0, bytes_accessed=1_100_000, transcendentals=0),
    )(diag_inv, row_v, row_u)


def prepare_kernel(ranks, tu, tv, sk, probe, upper, gram):
    rmax = sk.shape[1]
    t = pl.program_id(0)
    row = lax.broadcasted_iota(jnp.int32, (rmax, rmax), 0)
    col = lax.broadcasted_iota(jnp.int32, (rmax, rmax), 1)
    p = dot(tv[0], sk[...], 0, 0)
    p = jnp.where((row < ranks[t]) & (col < ranks[2 + t]), p, 0.0).astype(BF16)
    h = sum(dot(piece, p) for piece in pieces(dot(tu[0], tu[0], 0, 0), 3))
    probe[0] = p
    upper[0] = h
    gram[0] = 0.5 * sum(dot(p, piece, 0, 0) for piece in pieces(h, 3))


def prepare(ranks, trail_u, trail_v, sketch):
    width, rmax = sketch.shape
    square = lambda kind: jax.ShapeDtypeStruct((2, rmax, rmax), kind)
    tile = pl.BlockSpec((1, width, rmax), lambda t: (t, 0, 0))
    small = pl.BlockSpec((1, rmax, rmax), lambda t: (t, 0, 0))
    return pl.pallas_call(
        prepare_kernel,
        name="prepare",
        grid=(2,),
        out_shape=(square(BF16), square(F32), square(F32)),
        in_specs=[
            pl.BlockSpec(memory_space=pltpu.SMEM),
            tile,
            tile,
            pl.BlockSpec((width, rmax), lambda t: (0, 0)),
        ],
        out_specs=(small, small, small),
        compiler_params=pltpu.CompilerParams(vmem_limit_bytes=24 * 1024 * 1024),
        cost_estimate=pl.CostEstimate(
            flops=2_000_000_000, bytes_accessed=6_000_000, transcendentals=0
        ),
    )(ranks, trail_u, trail_v, sketch)


def reach_kernel(ranks, sk, up0, up1, up2, up3, out):
    part = up0.shape[0]
    total = None
    for k, block in enumerate((up0, up1, up2, up3)):
        at = pl.multiple_of(ranks[7 + k] * part, part)
        term = dot(block[...], sk[pl.ds(at, part)], 0, 0)
        total = term if total is None else total + term
    out[...] = total.astype(BF16)


def reach_of(ranks, sketch, uparts):
    rmax = sketch.shape[1]
    vmem = pl.BlockSpec(memory_space=pltpu.VMEM)
    return pl.pallas_call(
        reach_kernel,
        name="reach",
        out_shape=jax.ShapeDtypeStruct((rmax, rmax), BF16),
        in_specs=[pl.BlockSpec(memory_space=pltpu.SMEM)] + [vmem] * 5,
        out_specs=vmem,
        compiler_params=pltpu.CompilerParams(vmem_limit_bytes=12 * 1024 * 1024),
        cost_estimate=pl.CostEstimate(
            flops=300_000_000, bytes_accessed=2_200_000, transcendentals=0
        ),
    )(ranks, sketch, *uparts)


def tail_kernel(
    ranks,
    probe,
    upper,
    half,
    reach,
    gathered,
    vp0,
    vp1,
    vp2,
    vp3,
    up0,
    up1,
    up2,
    up3,
    trail_u,
    trail_v,
    fresh_u,
    fresh_v,
    dinv,
    vall,
    ui,
    uj,
    tu,
    tv,
    zs,
    bs,
    ou,
    ov,
    pv,
    hv,
    gv,
    rv,
    load_sem,
    out_sem,
):
    width, rmax = uj.shape
    part = width // 4
    smalls = (pv, hv, gv, rv)
    loads = []

    def load(src, dst):
        copy = pltpu.make_async_copy(src, dst, load_sem.at[len(loads)])
        copy.start()
        loads.append(copy)
        return copy

    def spots():
        return [pl.multiple_of(ranks[7 + k] * part, part) for k in range(4)]

    def load_d(q):
        chunks, rows = pl.ds(0, 2 * q + 2), pl.ds(part * q, part)
        return load(gathered.at[chunks, rows], dinv.at[chunks, rows])

    need_v = [load(gathered.at[8 + t], vall.at[:, pl.ds(rmax * t, rmax)]) for t in range(2)]
    for at, src in zip(spots(), (vp0, vp1, vp2, vp3)):
        need_v.append(load(src, vall.at[pl.ds(at, part), pl.ds(2 * rmax, rmax)]))
    need_d = [load_d(0), load_d(1)]
    for copy in need_v:
        copy.wait()
    need_d += [load_d(2), load_d(3)]
    coupling = [jnp.zeros((rmax, rmax), F32)] * 2
    for q in range(4):
        need_d[q].wait()
        if q == 1:
            need_u = [load(gathered.at[10 + t], ui.at[t]) for t in range(2)]
            need_u.append(load(trail_u, tu))
            need_u += [load(a, b) for a, b in zip((probe, upper, half, reach), smalls)]
        if q == 2:
            rest = [load(a, uj.at[pl.ds(at, part)]) for at, a in zip(spots(), (up0, up1, up2, up3))]
            rest.append(load(trail_v, tv))
        for n in range(2):
            at = part * q + rmax * n
            count = 2 * q + 1 + n
            lhs = jnp.concatenate([dinv[c, at : at + rmax] for c in range(count)], axis=1)
            w = dot(lhs, vall[: rmax * count]).astype(BF16)
            wj = w[:, 2 * rmax :]
            coupling = [
                coupling[t] + dot(w[:, rmax * t : rmax * (t + 1)], wj, 0, 0) for t in range(2)
            ]
    for copy in need_u:
        copy.wait()
    probe, upper, half, reach = smalls

    row = lax.broadcasted_iota(jnp.int32, (rmax, rmax), 0)
    col = lax.broadcasted_iota(jnp.int32, (rmax, rmax), 1)
    couplings, grams, probes, products = [], [], [], []
    for t in range(2):
        new_rank, row_rank, col_rank = ranks[2 + t], ranks[4 + t], ranks[6]
        keep = col < new_rank
        top = probe[t]
        c = jnp.where((row < row_rank) & (col < col_rank), coupling[t], 0.0).astype(BF16)
        bottom = jnp.where(keep, -dot(c, reach[...]), 0.0).astype(BF16)
        gur = pieces(dot(tu[t], ui[t], 0, 0), 3)
        grr = pieces(dot(ui[t], ui[t], 0, 0), 3)
        cross = sum(dot(piece, top, 0, 0) for piece in gur)
        own = sum(dot(piece, bottom) for piece in grr)
        mixed = pieces(cross + 0.5 * own, 3)
        gram = half[t] + sum(dot(bottom, piece, 0, 0) for piece in mixed)
        grams.append(gram + gram.T + jnp.where((row == col) & ~keep, 1.0, 0.0))
        couplings.append(c)
        probes.append(jnp.concatenate([top, bottom], axis=0))
        above = upper[t] + sum(dot(piece, bottom) for piece in gur[:2])
        products.append(pieces(jnp.concatenate([above, cross + own], axis=0), 2))
    inverses = inverse_factors(grams)
    for t in range(2):
        m = pieces(inverses[t] * math.sqrt(width), 2)
        zs[t] = (dot(probes[t], m[0], 1, 1) + dot(probes[t], m[1], 1, 1)).astype(BF16)
        g = products[t]
        back = dot(g[0], m[0], 1, 1) + (dot(g[0], m[1], 1, 1) + dot(g[1], m[0], 1, 1))
        top = jnp.where(row < ranks[t], back[:rmax], 0.0)
        bottom = -dot(couplings[t], back[rmax:].astype(BF16), 0, 0)
        bs[t] = (jnp.concatenate([top, bottom], axis=0) / width).astype(BF16)
    for copy in rest:
        copy.wait()

    copies = []
    for t in range(2):
        for n in range(4):
            rows = pl.ds(part * n, part)
            left = jnp.concatenate([tu[t, rows], ui[t, rows]], axis=1)
            ou[t, rows] = dot(left, zs[t]).astype(BF16)
            right = jnp.concatenate([tv[t, rows], uj[rows]], axis=1)
            ov[t, rows] = dot(right, bs[t]).astype(BF16)
            for src, dst in ((ou, fresh_u), (ov, fresh_v)):
                copy = pltpu.make_async_copy(
                    src.at[t, rows], dst.at[t, rows], out_sem.at[len(copies)]
                )
                copy.start()
                copies.append(copy)
    for copy in copies:
        copy.wait()


def tail(ranks, probe, upper, half, reach, gathered, vparts, uparts, trail_u, trail_v):
    _, width, rmax = trail_u.shape
    hbm = pl.BlockSpec(memory_space=pl.ANY)
    tile = jax.ShapeDtypeStruct(trail_u.shape, BF16)
    return pl.pallas_call(
        tail_kernel,
        name="tail",
        out_shape=(tile, tile),
        in_specs=[pl.BlockSpec(memory_space=pltpu.SMEM)] + [hbm] * 15,
        out_specs=(hbm, hbm),
        scratch_shapes=[
            pltpu.VMEM((8, width, rmax), BF16),
            pltpu.VMEM((width, 3 * rmax), BF16),
            pltpu.VMEM((2, width, rmax), BF16),
            pltpu.VMEM((width, rmax), BF16),
            pltpu.VMEM((2, width, rmax), BF16),
            pltpu.VMEM((2, width, rmax), BF16),
            pltpu.VMEM((2, 2 * rmax, rmax), BF16),
            pltpu.VMEM((2, 2 * rmax, rmax), BF16),
            pltpu.VMEM((2, width, rmax), BF16),
            pltpu.VMEM((2, width, rmax), BF16),
            pltpu.VMEM((2, rmax, rmax), BF16),
            pltpu.VMEM((2, rmax, rmax), F32),
            pltpu.VMEM((2, rmax, rmax), F32),
            pltpu.VMEM((rmax, rmax), BF16),
            pltpu.SemaphoreType.DMA((22,)),
            pltpu.SemaphoreType.DMA((16,)),
        ],
        compiler_params=pltpu.CompilerParams(vmem_limit_bytes=56 * 1024 * 1024),
        cost_estimate=pl.CostEstimate(
            flops=16_000_000_000, bytes_accessed=20_000_000, transcendentals=0
        ),
    )(ranks, probe, upper, half, reach, gathered, *vparts, *uparts, trail_u, trail_v)


def on_device(
    trail_u,
    trail_v,
    tile_rank,
    new_rank,
    row_u,
    row_v,
    row_rank,
    col_u,
    col_v,
    col_rank,
    diag_inv,
    sketch,
):
    trow, _, width, rmax = trail_u.shape
    x, z = lax.axis_index("x"), lax.axis_index("z")
    yc = lax.axis_index(("y", "c"))
    pcol = z * 8 + yc
    trail_u, trail_v = trail_u[:, 0], trail_v[:, 0]

    gathered = lax.all_gather(pack(diag_inv, row_v, row_u), ("z", "y", "c"), axis=1, tiled=True)

    times = (0, 2, 3, 1)
    swap = [(a * 4 + q, (times[a] ^ q) * 4 + a) for a in range(4) for q in range(4)]
    quarter = lax.ppermute(jnp.stack([col_v, col_u], axis=1), ("x", "z"), swap)
    quarter = lax.all_to_all(quarter, ("y", "c"), split_axis=0, concat_axis=2, tiled=True)[0]

    def spread(block):
        return [block] + [
            lax.ppermute(block, "x", [(a, (a + k) % 4) for a in range(4)]) for k in (1, 3, 2)
        ]

    vparts = spread(quarter[0])
    uparts = spread(quarter[1])
    vparts = [vparts[0], vparts[1], vparts[3], vparts[2]]
    uparts = [uparts[0], uparts[1], uparts[3], uparts[2]]

    own_row = lax.dynamic_slice_in_dim(row_rank, x * trow, trow)
    own_col = lax.dynamic_slice_in_dim(col_rank, pcol, 1)
    turn = jnp.array(times, jnp.int32)[z]
    quarters = [(turn ^ lax.rem(x + 4 - k, 4))[None] for k in range(4)]
    ranks = jnp.concatenate([tile_rank[:, 0], new_rank[:, 0], own_row, own_col] + quarters)
    probe, upper, half = prepare(ranks, trail_u, trail_v, sketch)
    reach = reach_of(ranks, sketch, uparts)
    fresh_u, fresh_v = tail(
        ranks, probe, upper, half, reach, gathered, vparts, uparts, trail_u, trail_v
    )
    return fresh_u[:, None], fresh_v[:, None]


def solution(mesh):
    split = Mesh(mesh.devices.reshape(4, 4, 4, 2), ("x", "z", "y", "c"))
    cols = ("z", "y", "c")
    tiles = P("x", cols, None, None)
    panel = P("x", cols, None)
    return jax.shard_map(
        on_device,
        mesh=split,
        in_specs=(
            tiles,
            tiles,
            P("x", cols),
            P("x", cols),
            panel,
            panel,
            P(),
            panel,
            panel,
            P(),
            P(cols, None),
            P(),
        ),
        out_specs=(tiles, tiles),
        check_vma=False,
    )
```

```python
import functools
import math

import jax
import jax.numpy as jnp
from jax import lax
from jax.experimental import pallas as pl
from jax.experimental.pallas import tpu as pltpu
from jax.sharding import Mesh, PartitionSpec as P

F32 = jnp.float32
BF16 = jnp.bfloat16
HALF = 128


def dot(a, b, ca=1, cb=0):
    return lax.dot_general(a, b, (((ca,), (cb,)), ((), ())), preferred_element_type=F32)


def pieces(x, count):
    out = []
    for _ in range(count):
        piece = x.astype(BF16)
        out.append(piece)
        x = x - piece.astype(F32)
    return out


def joined(a, b, pairs, ca=1, cb=0):
    left = jnp.concatenate([a[i] for i, _ in pairs], axis=ca)
    right = jnp.concatenate([b[j] for _, j in pairs], axis=cb)
    return dot(left, right, ca, cb)


ONE = ((0, 0), (1, 0), (2, 0))
SIX = ((0, 0), (0, 1), (1, 0), (1, 1), (0, 2), (2, 0))


def exact(a, b, ca=1, cb=0):
    return joined(pieces(a, 3), pieces(b, 3), SIX, ca, cb)


def tree(terms):
    while len(terms) > 1:
        terms = [a + b for a, b in zip(terms[::2], terms[1::2])] + (terms[-1:] if len(terms) % 2 else [])
    return terms[0]

def eliminate(blocks):
    n = HALF
    groups = n // 8
    lane = lax.broadcasted_iota(jnp.int32, (8, n), 1)
    sub = lax.broadcasted_iota(jnp.int32, (8, n), 0)
    spread = lambda v, r: jnp.broadcast_to(v[r : r + 1], (8, n))
    tiles = [[m[8 * i : 8 * i + 8] for i in range(groups)] for m in blocks]

    def column(v, at):
        return jnp.broadcast_to(jnp.sum(jnp.where(lane == at, v, 0.0), axis=1, keepdims=True), (8, n))

    for g in range(groups):
        panel = (lane >= 8 * g) & (lane < 8 * g + 8)
        for x in tiles:
            cols = [[column(x[i], 8 * g + j) for j in range(8)] for i in range(g, groups)]
            top, own, kept = x[g], list(cols[0]), x[g]
            raw, fresh = list(own), top
            for m in range(0, 8, 2):
                c0, c1 = own[m], own[m + 1]
                a, b, c = spread(raw[m], m), spread(raw[m + 1], m), spread(raw[m + 1], m + 1)
                inv = pl.reciprocal(a * c - b * b, approx=True)
                upper, lower = sub == m, sub == m + 1
                for j in range(m + 2, 8):
                    s0, s1 = spread(raw[j], m), spread(raw[j], m + 1)
                    h0, h1 = c * s0 - b * s1, a * s1 - b * s0
                    raw[j] = own[j] - inv * (c0 * h0 + c1 * h1)
                    own[j] = jnp.where(upper, inv * h0, jnp.where(lower, inv * h1, raw[j]))
                k = 8 * g + m
                first, second = lane == k, lane == k + 1
                if m:
                    kept = jnp.where(upper | lower, fresh, kept)
                r0, r1 = spread(fresh, m), spread(fresh, m + 1)
                r0 = jnp.where(first, 1.0, jnp.where(second, 0.0, r0))
                r1 = jnp.where(second, 1.0, jnp.where(first, 0.0, r1))
                h0, h1 = c * r0 - b * r1, a * r1 - b * r0
                fresh = jnp.where(first | second, 0.0, top) - inv * (c0 * h0 + c1 * h1)
                top = jnp.where(upper, inv * h0, jnp.where(lower, inv * h1, fresh))
            x[g] = kept
            if g + 1 < groups:
                solved = [spread(top, m) for m in range(8)]
                for t in range(1, groups - g):
                    terms = [cols[t][m] * solved[m] for m in range(8)]
                    x[g + t] = jnp.where(panel, 0.0, x[g + t]) - tree(terms)
    odd = (sub % 2) == 1
    out = []
    for x in tiles:
        done = []
        for i in range(groups):
            row = sub + 8 * i
            pivot_start = row - row % 2
            here = jnp.sum(jnp.where(lane == row, x[i], 0.0), axis=1, keepdims=True)
            above = jnp.sum(jnp.where((lane == row + 1) & ~odd, x[i], 0.0), axis=1, keepdims=True)
            here = jnp.broadcast_to(here, (8, n))
            above = jnp.broadcast_to(above, (8, n))
            unit = jnp.where(lane < pivot_start, x[i], jnp.where(lane == row, 1.0, 0.0))
            ratio = jnp.where(odd, pltpu.roll(above / here, 1, axis=0), 0.0)
            above = jnp.where(odd, pltpu.roll(above, 1, axis=0), 0.0)
            scale = lax.rsqrt(here - ratio * above)
            done.append((unit - ratio * pltpu.roll(unit, 1, axis=0)) * scale)
        out.append(jnp.concatenate(done, axis=0))
    return out


def inverse_factors(grams):
    h = HALF
    n = 2 * h
    diagonal = lax.broadcasted_iota(jnp.int32, (n, n), 0) == lax.broadcasted_iota(
        jnp.int32, (n, n), 1
    )
    scales, scaled = [], []
    for g in grams:
        kept = jnp.where(diagonal, g, 0.0)
        across = lax.rsqrt(jnp.sum(kept, axis=0, keepdims=True))
        down = lax.rsqrt(jnp.sum(kept, axis=1, keepdims=True))
        scales.append(across)
        scaled.append((g * down) * across)
    m1 = eliminate([g[:h, :h] for g in scaled])
    u12 = [exact(m, g[:h, h:]) for m, g in zip(m1, scaled)]
    m2 = eliminate([g[h:, h:] - exact(u, u, 0, 0) for u, g in zip(u12, scaled)])
    m21 = [-exact(b, exact(u, a, 0, 0)) for a, b, u in zip(m1, m2, u12)]
    zero = jnp.zeros((h, h), F32)
    return [
        jnp.concatenate(
            [jnp.concatenate([a, zero], axis=1), jnp.concatenate([c, b], axis=1)], axis=0
        )
        * scale
        for a, b, c, scale in zip(m1, m2, m21, scales)
    ]


def pack_kernel(diag, row_v, row_u, out):
    chunks = out.shape[0] - 4
    rmax = out.shape[2]
    for c in range(chunks):
        out[c] = diag[:, rmax * c : rmax * (c + 1)].astype(BF16)
    out[chunks : chunks + 2] = row_v[...]
    out[chunks + 2 :] = row_u[...]


def pack(diag_inv, row_v, row_u):
    count, slab, rmax = row_v.shape
    chunks = diag_inv.shape[1] // rmax
    return pl.pallas_call(
        pack_kernel,
        name="pack",
        out_shape=jax.ShapeDtypeStruct((chunks + 2 * count, slab, rmax), BF16),
        cost_estimate=pl.CostEstimate(flops=0, bytes_accessed=1_100_000, transcendentals=0),
    )(diag_inv, row_v, row_u)


def prepare_kernel(ranks, tu, tv, sk, probe, upper, gram):
    rmax = sk.shape[1]
    t = pl.program_id(0)
    row = lax.broadcasted_iota(jnp.int32, (rmax, rmax), 0)
    col = lax.broadcasted_iota(jnp.int32, (rmax, rmax), 1)
    p = dot(tv[0], sk[...], 0, 0)
    p = jnp.where((row < ranks[t]) & (col < ranks[2 + t]), p, 0.0).astype(BF16)
    h = sum(dot(piece, p) for piece in pieces(dot(tu[0], tu[0], 0, 0), 3))
    probe[0] = p
    upper[0] = h
    gram[0] = 0.5 * sum(dot(p, piece, 0, 0) for piece in pieces(h, 3))


def prepare(ranks, trail_u, trail_v, sketch):
    width, rmax = sketch.shape
    square = lambda kind: jax.ShapeDtypeStruct((2, rmax, rmax), kind)
    tile = pl.BlockSpec((1, width, rmax), lambda t: (t, 0, 0))
    small = pl.BlockSpec((1, rmax, rmax), lambda t: (t, 0, 0))
    return pl.pallas_call(
        prepare_kernel,
        name="prepare",
        grid=(2,),
        out_shape=(square(BF16), square(F32), square(F32)),
        in_specs=[
            pl.BlockSpec(memory_space=pltpu.SMEM),
            tile,
            tile,
            pl.BlockSpec((width, rmax), lambda t: (0, 0)),
        ],
        out_specs=(small, small, small),
        compiler_params=pltpu.CompilerParams(vmem_limit_bytes=24 * 1024 * 1024),
        cost_estimate=pl.CostEstimate(
            flops=2_000_000_000, bytes_accessed=6_000_000, transcendentals=0
        ),
    )(ranks, trail_u, trail_v, sketch)


def reach_kernel(ranks, sk, up0, up1, up2, up3, out):
    part = up0.shape[0]
    total = None
    for k, block in enumerate((up0, up1, up2, up3)):
        at = pl.multiple_of(ranks[7 + k] * part, part)
        term = dot(block[...], sk[pl.ds(at, part)], 0, 0)
        total = term if total is None else total + term
    out[...] = total.astype(BF16)


def reach_of(ranks, sketch, uparts):
    rmax = sketch.shape[1]
    vmem = pl.BlockSpec(memory_space=pltpu.VMEM)
    return pl.pallas_call(
        reach_kernel,
        name="reach",
        out_shape=jax.ShapeDtypeStruct((rmax, rmax), BF16),
        in_specs=[pl.BlockSpec(memory_space=pltpu.SMEM)] + [vmem] * 5,
        out_specs=vmem,
        compiler_params=pltpu.CompilerParams(vmem_limit_bytes=12 * 1024 * 1024),
        cost_estimate=pl.CostEstimate(
            flops=300_000_000, bytes_accessed=2_200_000, transcendentals=0
        ),
    )(ranks, sketch, *uparts)


def tail_kernel(
    ranks,
    probe,
    upper,
    half,
    reach,
    gathered,
    vp0,
    vp1,
    vp2,
    vp3,
    up0,
    up1,
    up2,
    up3,
    trail_u,
    trail_v,
    fresh_u,
    fresh_v,
    dinv,
    vall,
    wall,
    ui,
    uj,
    tu,
    tv,
    zs,
    bs,
    ou,
    ov,
    pv,
    hv,
    gv,
    rv,
    ps,
    load_sem,
    out_sem,
):
    width, rmax = uj.shape
    part = width // 4
    smalls = (pv, hv, gv, rv)
    loads = []

    def load(src, dst):
        copy = pltpu.make_async_copy(src, dst, load_sem.at[len(loads)])
        copy.start()
        loads.append(copy)
        return copy

    def spots():
        return [pl.multiple_of(ranks[7 + k] * part, part) for k in range(4)]

    def load_d(q):
        chunks, rows = pl.ds(0, 2 * q + 2), pl.ds(part * q, part)
        return load(gathered.at[chunks, rows], dinv.at[chunks, rows])

    def load_quarter(q):
        rows = pl.ds(part * q, part)
        copies = [
            load(gathered.at[8 + t, rows], vall.at[rows, pl.ds(rmax * t, rmax)]) for t in range(2)
        ]
        chunks = pl.ds(0, 2 * q + 2)
        return copies + [load(gathered.at[chunks, rows], dinv.at[chunks, rows])]

    need_vj = [
        load(a, vall.at[pl.ds(at, part), pl.ds(2 * rmax, rmax)])
        for at, a in zip(spots(), (vp0, vp1, vp2, vp3))
    ]
    need = [load_quarter(0), load_quarter(1)]
    need_u = [load(gathered.at[10 + t], ui.at[t]) for t in range(2)]
    need_u.append(load(trail_u, tu))
    need += [load_quarter(2), load_quarter(3)]
    need_smalls = [load(a, b) for a, b in zip((probe, upper, half, reach), smalls)]
    rest = [load(a, uj.at[pl.ds(at, part)]) for at, a in zip(spots(), (up0, up1, up2, up3))]
    rest.append(load(trail_v, tv))
    for copy in need_vj:
        copy.wait()
    for q in range(4):
        for copy in need[q]:
            copy.wait()
        for n in range(2):
            at = part * q + rmax * n
            count = 2 * q + 1 + n
            lhs = jnp.concatenate([dinv[c, at : at + rmax] for c in range(count)], axis=1)
            wall[at : at + rmax] = dot(lhs, vall[: rmax * count]).astype(BF16)
        if q == 1:
            for copy in need_u:
                copy.wait()
            for t in range(2):
                sides = jnp.concatenate([tu[t], ui[t]], axis=1)
                ps[t] = dot(ui[t], sides, 0, 0)
    for copy in need_smalls:
        copy.wait()
    probe, upper, half, reach = smalls
    parts = [(pieces(ps[t, :, :rmax], 3), pieces(ps[t, :, rmax:], 3)) for t in range(2)]
    crosses = [joined(parts[t][0], [probe[t]], ONE) for t in range(2)]
    coupling = dot(wall[:, : 2 * rmax], wall[:, 2 * rmax :], 0, 0)

    row = lax.broadcasted_iota(jnp.int32, (rmax, rmax), 0)
    col = lax.broadcasted_iota(jnp.int32, (rmax, rmax), 1)
    couplings, grams, probes, products = [], [], [], []
    for t in range(2):
        new_rank, row_rank, col_rank = ranks[2 + t], ranks[4 + t], ranks[6]
        keep = col < new_rank
        top = probe[t]
        c = coupling[rmax * t : rmax * (t + 1)]
        c = jnp.where((row < row_rank) & (col < col_rank), c, 0.0).astype(BF16)
        bottom = jnp.where(keep, -dot(c, reach[...]), 0.0).astype(BF16)
        gru, grr = parts[t]
        cross = crosses[t]
        own = joined(grr, [bottom], ONE)
        mixed = pieces(cross + 0.5 * own, 3)
        gram = half[t] + joined([bottom], mixed, ((0, 0), (0, 1), (0, 2)), 0, 0)
        grams.append(gram + gram.T + jnp.where((row == col) & ~keep, 1.0, 0.0))
        couplings.append(c)
        probes.append(jnp.concatenate([top, bottom], axis=0))
        above = upper[t] + joined(gru, [bottom], ONE[:2], 0, 0)
        products.append(pieces(jnp.concatenate([above, cross + own], axis=0), 2))
    inverses = inverse_factors(grams)
    for t in range(2):
        m = pieces(inverses[t] * math.sqrt(width), 2)
        zs[t] = joined([probes[t]], m, ((0, 0), (0, 1)), 1, 1).astype(BF16)
        back = joined(products[t], m, ((0, 0), (0, 1), (1, 0)), 1, 1)
        top = jnp.where(row < ranks[t], back[:rmax], 0.0)
        bottom = -dot(couplings[t], back[rmax:].astype(BF16), 0, 0)
        bs[t] = (jnp.concatenate([top, bottom], axis=0) / width).astype(BF16)
    for copy in rest:
        copy.wait()

    copies = []
    for t in range(2):
        for n in range(4):
            rows = pl.ds(part * n, part)
            left = jnp.concatenate([tu[t, rows], ui[t, rows]], axis=1)
            ou[t, rows] = dot(left, zs[t]).astype(BF16)
            right = jnp.concatenate([tv[t, rows], uj[rows]], axis=1)
            ov[t, rows] = dot(right, bs[t]).astype(BF16)
            for src, dst in ((ou, fresh_u), (ov, fresh_v)):
                copy = pltpu.make_async_copy(
                    src.at[t, rows], dst.at[t, rows], out_sem.at[len(copies)]
                )
                copy.start()
                copies.append(copy)
    for copy in copies:
        copy.wait()


def tail(ranks, probe, upper, half, reach, gathered, vparts, uparts, trail_u, trail_v):
    _, width, rmax = trail_u.shape
    hbm = pl.BlockSpec(memory_space=pl.ANY)
    tile = jax.ShapeDtypeStruct(trail_u.shape, BF16)
    return pl.pallas_call(
        tail_kernel,
        name="tail",
        out_shape=(tile, tile),
        in_specs=[pl.BlockSpec(memory_space=pltpu.SMEM)] + [hbm] * 15,
        out_specs=(hbm, hbm),
        scratch_shapes=[
            pltpu.VMEM((8, width, rmax), BF16),
            pltpu.VMEM((width, 3 * rmax), BF16),
            pltpu.VMEM((width, 3 * rmax), BF16),
            pltpu.VMEM((2, width, rmax), BF16),
            pltpu.VMEM((width, rmax), BF16),
            pltpu.VMEM((2, width, rmax), BF16),
            pltpu.VMEM((2, width, rmax), BF16),
            pltpu.VMEM((2, 2 * rmax, rmax), BF16),
            pltpu.VMEM((2, 2 * rmax, rmax), BF16),
            pltpu.VMEM((2, width, rmax), BF16),
            pltpu.VMEM((2, width, rmax), BF16),
            pltpu.VMEM((2, rmax, rmax), BF16),
            pltpu.VMEM((2, rmax, rmax), F32),
            pltpu.VMEM((2, rmax, rmax), F32),
            pltpu.VMEM((rmax, rmax), BF16),
            pltpu.VMEM((2, rmax, 2 * rmax), F32),
            pltpu.SemaphoreType.DMA((28,)),
            pltpu.SemaphoreType.DMA((16,)),
        ],
        compiler_params=pltpu.CompilerParams(vmem_limit_bytes=56 * 1024 * 1024),
        cost_estimate=pl.CostEstimate(
            flops=16_000_000_000, bytes_accessed=20_000_000, transcendentals=0
        ),
    )(ranks, probe, upper, half, reach, gathered, *vparts, *uparts, trail_u, trail_v)


def on_device(
    trail_u,
    trail_v,
    tile_rank,
    new_rank,
    row_u,
    row_v,
    row_rank,
    col_u,
    col_v,
    col_rank,
    diag_inv,
    sketch,
):
    trow, _, width, rmax = trail_u.shape
    x, z = lax.axis_index("x"), lax.axis_index("z")
    yc = lax.axis_index(("y", "c"))
    pcol = z * 8 + yc
    trail_u, trail_v = trail_u[:, 0], trail_v[:, 0]

    gathered = lax.all_gather(pack(diag_inv, row_v, row_u), ("z", "y", "c"), axis=1, tiled=True)

    times = (0, 2, 3, 1)
    swap = [(a * 4 + q, (times[a] ^ q) * 4 + a) for a in range(4) for q in range(4)]
    quarter = lax.ppermute(jnp.stack([col_v, col_u], axis=1), ("x", "z"), swap)
    quarter = lax.all_to_all(quarter, ("y", "c"), split_axis=0, concat_axis=2, tiled=True)[0]

    def spread(block):
        return [block] + [
            lax.ppermute(block, "x", [(a, (a + k) % 4) for a in range(4)]) for k in (1, 3, 2)
        ]

    vparts = spread(quarter[0])
    uparts = spread(quarter[1])
    vparts = [vparts[0], vparts[1], vparts[3], vparts[2]]
    uparts = [uparts[0], uparts[1], uparts[3], uparts[2]]

    own_row = lax.dynamic_slice_in_dim(row_rank, x * trow, trow)
    own_col = lax.dynamic_slice_in_dim(col_rank, pcol, 1)
    turn = jnp.array(times, jnp.int32)[z]
    quarters = [(turn ^ lax.rem(x + 4 - k, 4))[None] for k in range(4)]
    ranks = jnp.concatenate([tile_rank[:, 0], new_rank[:, 0], own_row, own_col] + quarters)
    probe, upper, half = prepare(ranks, trail_u, trail_v, sketch)
    reach = reach_of(ranks, sketch, uparts)
    fresh_u, fresh_v = tail(
        ranks, probe, upper, half, reach, gathered, vparts, uparts, trail_u, trail_v
    )
    return fresh_u[:, None], fresh_v[:, None]


def solution(mesh):
    split = Mesh(mesh.devices.reshape(4, 4, 4, 2), ("x", "z", "y", "c"))
    cols = ("z", "y", "c")
    tiles = P("x", cols, None, None)
    panel = P("x", cols, None)
    return jax.shard_map(
        on_device,
        mesh=split,
        in_specs=(
            tiles,
            tiles,
            P("x", cols),
            P("x", cols),
            panel,
            panel,
            P(),
            panel,
            panel,
            P(),
            P(cols, None),
            P(),
        ),
        out_specs=(tiles, tiles),
        check_vma=False,
    )
```

```python
import functools
import math

import jax
import jax.numpy as jnp
from jax import lax
from jax.experimental import pallas as pl
from jax.experimental.pallas import tpu as pltpu
from jax.sharding import Mesh, PartitionSpec as P

F32 = jnp.float32
BF16 = jnp.bfloat16
HALF = 128


def dot(a, b, ca=1, cb=0):
    return lax.dot_general(a, b, (((ca,), (cb,)), ((), ())), preferred_element_type=F32)


def pieces(x, count):
    out = []
    for _ in range(count):
        piece = x.astype(BF16)
        out.append(piece)
        x = x - piece.astype(F32)
    return out


def joined(a, b, pairs, ca=1, cb=0):
    left = jnp.concatenate([a[i] for i, _ in pairs], axis=ca)
    right = jnp.concatenate([b[j] for _, j in pairs], axis=cb)
    return dot(left, right, ca, cb)


ONE = ((0, 0), (1, 0), (2, 0))
SIX = ((0, 0), (0, 1), (1, 0), (1, 1), (0, 2), (2, 0))


def exact(a, b, ca=1, cb=0):
    return joined(pieces(a, 3), pieces(b, 3), SIX, ca, cb)


def tree(terms):
    while len(terms) > 1:
        terms = [a + b for a, b in zip(terms[::2], terms[1::2])] + (terms[-1:] if len(terms) % 2 else [])
    return terms[0]

def eliminate(blocks):
    n = HALF
    groups = n // 8
    lane = lax.broadcasted_iota(jnp.int32, (8, n), 1)
    sub = lax.broadcasted_iota(jnp.int32, (8, n), 0)
    spread = lambda v, r: jnp.broadcast_to(v[r : r + 1], (8, n))
    tiles = [[m[8 * i : 8 * i + 8] for i in range(groups)] for m in blocks]

    def column(v, at):
        return jnp.broadcast_to(jnp.sum(jnp.where(lane == at, v, 0.0), axis=1, keepdims=True), (8, n))

    for g in range(groups):
        panel = (lane >= 8 * g) & (lane < 8 * g + 8)
        for x in tiles:
            cols = [[column(x[i], 8 * g + j) for j in range(8)] for i in range(g, groups)]
            top, own, kept = x[g], list(cols[0]), x[g]
            raw, fresh = list(own), top
            for m in range(0, 8, 2):
                c0, c1 = own[m], own[m + 1]
                a, b, c = spread(raw[m], m), spread(raw[m + 1], m), spread(raw[m + 1], m + 1)
                inv = pl.reciprocal(a * c - b * b, approx=True)
                upper, lower = sub == m, sub == m + 1
                for j in range(m + 2, 8):
                    s0, s1 = spread(raw[j], m), spread(raw[j], m + 1)
                    h0, h1 = c * s0 - b * s1, a * s1 - b * s0
                    raw[j] = own[j] - inv * (c0 * h0 + c1 * h1)
                    own[j] = jnp.where(upper, inv * h0, jnp.where(lower, inv * h1, raw[j]))
                k = 8 * g + m
                first, second = lane == k, lane == k + 1
                if m:
                    kept = jnp.where(upper | lower, fresh, kept)
                r0, r1 = spread(fresh, m), spread(fresh, m + 1)
                r0 = jnp.where(first, 1.0, jnp.where(second, 0.0, r0))
                r1 = jnp.where(second, 1.0, jnp.where(first, 0.0, r1))
                h0, h1 = c * r0 - b * r1, a * r1 - b * r0
                fresh = jnp.where(first | second, 0.0, top) - inv * (c0 * h0 + c1 * h1)
                top = jnp.where(upper, inv * h0, jnp.where(lower, inv * h1, fresh))
            x[g] = kept
            if g + 1 < groups:
                solved = [spread(top, m) for m in range(8)]
                for t in range(1, groups - g):
                    terms = [cols[t][m] * solved[m] for m in range(8)]
                    x[g + t] = jnp.where(panel, 0.0, x[g + t]) - tree(terms)
    odd = (sub % 2) == 1
    out = []
    for x in tiles:
        done = []
        for i in range(groups):
            row = sub + 8 * i
            pivot_start = row - row % 2
            here = jnp.sum(jnp.where(lane == row, x[i], 0.0), axis=1, keepdims=True)
            above = jnp.sum(jnp.where((lane == row + 1) & ~odd, x[i], 0.0), axis=1, keepdims=True)
            here = jnp.broadcast_to(here, (8, n))
            above = jnp.broadcast_to(above, (8, n))
            unit = jnp.where(lane < pivot_start, x[i], jnp.where(lane == row, 1.0, 0.0))
            ratio = jnp.where(odd, pltpu.roll(above / here, 1, axis=0), 0.0)
            above = jnp.where(odd, pltpu.roll(above, 1, axis=0), 0.0)
            scale = lax.rsqrt(here - ratio * above)
            done.append((unit - ratio * pltpu.roll(unit, 1, axis=0)) * scale)
        out.append(jnp.concatenate(done, axis=0))
    return out


def inverse_factors(grams):
    h = HALF
    n = 2 * h
    diagonal = lax.broadcasted_iota(jnp.int32, (n, n), 0) == lax.broadcasted_iota(
        jnp.int32, (n, n), 1
    )
    scales, scaled = [], []
    for g in grams:
        kept = jnp.where(diagonal, g, 0.0)
        across = lax.rsqrt(jnp.sum(kept, axis=0, keepdims=True))
        down = lax.rsqrt(jnp.sum(kept, axis=1, keepdims=True))
        scales.append(across)
        scaled.append((g * down) * across)
    m1 = eliminate([g[:h, :h] for g in scaled])
    u12 = [exact(m, g[:h, h:]) for m, g in zip(m1, scaled)]
    m2 = eliminate([g[h:, h:] - exact(u, u, 0, 0) for u, g in zip(u12, scaled)])
    m21 = [-exact(b, exact(u, a, 0, 0)) for a, b, u in zip(m1, m2, u12)]
    zero = jnp.zeros((h, h), F32)
    return [
        jnp.concatenate(
            [jnp.concatenate([a, zero], axis=1), jnp.concatenate([c, b], axis=1)], axis=0
        )
        * scale
        for a, b, c, scale in zip(m1, m2, m21, scales)
    ]


def pack_kernel(diag, row_v, row_u, out):
    chunks = out.shape[0] - 4
    rmax = out.shape[2]
    for c in range(chunks):
        out[c] = diag[:, rmax * c : rmax * (c + 1)].astype(BF16)
    out[chunks : chunks + 2] = row_v[...]
    out[chunks + 2 :] = row_u[...]


def pack(diag_inv, row_v, row_u):
    count, slab, rmax = row_v.shape
    chunks = diag_inv.shape[1] // rmax
    return pl.pallas_call(
        pack_kernel,
        name="pack",
        out_shape=jax.ShapeDtypeStruct((chunks + 2 * count, slab, rmax), BF16),
        cost_estimate=pl.CostEstimate(flops=0, bytes_accessed=1_100_000, transcendentals=0),
    )(diag_inv, row_v, row_u)


def prepare_kernel(ranks, tu, tv, sk, probe, upper, gram):
    rmax = sk.shape[1]
    t = pl.program_id(0)
    row = lax.broadcasted_iota(jnp.int32, (rmax, rmax), 0)
    col = lax.broadcasted_iota(jnp.int32, (rmax, rmax), 1)
    p = dot(tv[0], sk[...], 0, 0)
    p = jnp.where((row < ranks[t]) & (col < ranks[2 + t]), p, 0.0).astype(BF16)
    h = sum(dot(piece, p) for piece in pieces(dot(tu[0], tu[0], 0, 0), 3))
    probe[0] = p
    upper[0] = h
    gram[0] = 0.5 * sum(dot(p, piece, 0, 0) for piece in pieces(h, 3))


def prepare(ranks, trail_u, trail_v, sketch):
    width, rmax = sketch.shape
    square = lambda kind: jax.ShapeDtypeStruct((2, rmax, rmax), kind)
    tile = pl.BlockSpec((1, width, rmax), lambda t: (t, 0, 0))
    small = pl.BlockSpec((1, rmax, rmax), lambda t: (t, 0, 0))
    return pl.pallas_call(
        prepare_kernel,
        name="prepare",
        grid=(2,),
        out_shape=(square(BF16), square(F32), square(F32)),
        in_specs=[
            pl.BlockSpec(memory_space=pltpu.SMEM),
            tile,
            tile,
            pl.BlockSpec((width, rmax), lambda t: (0, 0)),
        ],
        out_specs=(small, small, small),
        compiler_params=pltpu.CompilerParams(vmem_limit_bytes=24 * 1024 * 1024),
        cost_estimate=pl.CostEstimate(
            flops=2_000_000_000, bytes_accessed=6_000_000, transcendentals=0
        ),
    )(ranks, trail_u, trail_v, sketch)


def reach_kernel(ranks, sk, up0, up1, up2, up3, out):
    part = up0.shape[0]
    total = None
    for k, block in enumerate((up0, up1, up2, up3)):
        at = pl.multiple_of(ranks[7 + k] * part, part)
        term = dot(block[...], sk[pl.ds(at, part)], 0, 0)
        total = term if total is None else total + term
    out[...] = total.astype(BF16)


def reach_of(ranks, sketch, uparts):
    rmax = sketch.shape[1]
    vmem = pl.BlockSpec(memory_space=pltpu.VMEM)
    return pl.pallas_call(
        reach_kernel,
        name="reach",
        out_shape=jax.ShapeDtypeStruct((rmax, rmax), BF16),
        in_specs=[pl.BlockSpec(memory_space=pltpu.SMEM)] + [vmem] * 5,
        out_specs=vmem,
        compiler_params=pltpu.CompilerParams(vmem_limit_bytes=12 * 1024 * 1024),
        cost_estimate=pl.CostEstimate(
            flops=300_000_000, bytes_accessed=2_200_000, transcendentals=0
        ),
    )(ranks, sketch, *uparts)


def tail_kernel(
    ranks,
    probe,
    upper,
    half,
    reach,
    gathered,
    vp0,
    vp1,
    vp2,
    vp3,
    up0,
    up1,
    up2,
    up3,
    trail_u,
    trail_v,
    fresh_u,
    fresh_v,
    dinv,
    vall,
    wall,
    ui,
    uj,
    tu,
    tv,
    zs,
    bs,
    ou,
    ov,
    pv,
    hv,
    gv,
    rv,
    ps,
    load_sem,
    out_sem,
):
    width, rmax = uj.shape
    part = width // 4
    smalls = (pv, hv, gv, rv)
    loads = []

    def load(src, dst):
        copy = pltpu.make_async_copy(src, dst, load_sem.at[len(loads)])
        copy.start()
        loads.append(copy)
        return copy

    def spots():
        return [pl.multiple_of(ranks[7 + k] * part, part) for k in range(4)]

    def load_d(q):
        chunks, rows = pl.ds(0, 2 * q + 2), pl.ds(part * q, part)
        return load(gathered.at[chunks, rows], dinv.at[chunks, rows])

    def load_quarter(q):
        rows = pl.ds(part * q, part)
        copies = [
            load(gathered.at[8 + t, rows], vall.at[rows, pl.ds(rmax * t, rmax)]) for t in range(2)
        ]
        for n in range(2):
            chunks, block = pl.ds(0, 2 * q + 1 + n), pl.ds(part * q + rmax * n, rmax)
            copies.append(load(gathered.at[chunks, block], dinv.at[chunks, block]))
        return copies

    need_vj = [
        load(a, vall.at[pl.ds(at, part), pl.ds(2 * rmax, rmax)])
        for at, a in zip(spots(), (vp0, vp1, vp2, vp3))
    ]
    need = [load_quarter(0), load_quarter(1)]
    need_u = [load(gathered.at[10 + t], ui.at[t]) for t in range(2)]
    need_u.append(load(trail_u, tu))
    need += [load_quarter(2), load_quarter(3)]
    for copy in need_vj:
        copy.wait()
    for q in range(4):
        for copy in need[q]:
            copy.wait()
        if q == 1:
            need_smalls = [load(a, b) for a, b in zip((probe, upper, half, reach), smalls)]
        if q == 2:
            rest = [load(a, uj.at[pl.ds(at, part)]) for at, a in zip(spots(), (up0, up1, up2, up3))]
            rest.append(load(trail_v, tv))
        for n in range(2):
            at = part * q + rmax * n
            count = 2 * q + 1 + n
            lhs = jnp.concatenate([dinv[c, at : at + rmax] for c in range(count)], axis=1)
            wall[at : at + rmax] = dot(lhs, vall[: rmax * count]).astype(BF16)
        if q == 1:
            for copy in need_u:
                copy.wait()
            for t in range(2):
                sides = jnp.concatenate([tu[t], ui[t]], axis=1)
                ps[t] = dot(ui[t], sides, 0, 0)
    for copy in need_smalls:
        copy.wait()
    probe, upper, half, reach = smalls
    parts = [(pieces(ps[t, :, :rmax], 3), pieces(ps[t, :, rmax:], 3)) for t in range(2)]
    crosses = [joined(parts[t][0], [probe[t]], ONE) for t in range(2)]
    coupling = dot(wall[:, : 2 * rmax], wall[:, 2 * rmax :], 0, 0)

    row = lax.broadcasted_iota(jnp.int32, (rmax, rmax), 0)
    col = lax.broadcasted_iota(jnp.int32, (rmax, rmax), 1)
    couplings, grams, probes, products = [], [], [], []
    for t in range(2):
        new_rank, row_rank, col_rank = ranks[2 + t], ranks[4 + t], ranks[6]
        keep = col < new_rank
        top = probe[t]
        c = coupling[rmax * t : rmax * (t + 1)]
        c = jnp.where((row < row_rank) & (col < col_rank), c, 0.0).astype(BF16)
        bottom = jnp.where(keep, -dot(c, reach[...]), 0.0).astype(BF16)
        gru, grr = parts[t]
        cross = crosses[t]
        own = joined(grr, [bottom], ONE)
        mixed = pieces(cross + 0.5 * own, 3)
        gram = half[t] + joined([bottom], mixed, ((0, 0), (0, 1), (0, 2)), 0, 0)
        grams.append(gram + gram.T + jnp.where((row == col) & ~keep, 1.0, 0.0))
        couplings.append(c)
        probes.append(jnp.concatenate([top, bottom], axis=0))
        above = upper[t] + joined(gru, [bottom], ONE[:2], 0, 0)
        products.append(pieces(jnp.concatenate([above, cross + own], axis=0), 2))
    inverses = inverse_factors(grams)
    for t in range(2):
        m = pieces(inverses[t] * math.sqrt(width), 2)
        zs[t] = joined([probes[t]], m, ((0, 0), (0, 1)), 1, 1).astype(BF16)
        back = joined(products[t], m, ((0, 0), (0, 1), (1, 0)), 1, 1)
        top = jnp.where(row < ranks[t], back[:rmax], 0.0)
        bottom = -dot(couplings[t], back[rmax:].astype(BF16), 0, 0)
        bs[t] = (jnp.concatenate([top, bottom], axis=0) / width).astype(BF16)
    for copy in rest:
        copy.wait()

    copies = []
    for t in range(2):
        for n in range(4):
            rows = pl.ds(part * n, part)
            left = jnp.concatenate([tu[t, rows], ui[t, rows]], axis=1)
            ou[t, rows] = dot(left, zs[t]).astype(BF16)
            right = jnp.concatenate([tv[t, rows], uj[rows]], axis=1)
            ov[t, rows] = dot(right, bs[t]).astype(BF16)
            for src, dst in ((ou, fresh_u), (ov, fresh_v)):
                copy = pltpu.make_async_copy(
                    src.at[t, rows], dst.at[t, rows], out_sem.at[len(copies)]
                )
                copy.start()
                copies.append(copy)
    for copy in copies:
        copy.wait()


def tail(ranks, probe, upper, half, reach, gathered, vparts, uparts, trail_u, trail_v):
    _, width, rmax = trail_u.shape
    hbm = pl.BlockSpec(memory_space=pl.ANY)
    tile = jax.ShapeDtypeStruct(trail_u.shape, BF16)
    return pl.pallas_call(
        tail_kernel,
        name="tail",
        out_shape=(tile, tile),
        in_specs=[pl.BlockSpec(memory_space=pltpu.SMEM)] + [hbm] * 15,
        out_specs=(hbm, hbm),
        scratch_shapes=[
            pltpu.VMEM((8, width, rmax), BF16),
            pltpu.VMEM((width, 3 * rmax), BF16),
            pltpu.VMEM((width, 3 * rmax), BF16),
            pltpu.VMEM((2, width, rmax), BF16),
            pltpu.VMEM((width, rmax), BF16),
            pltpu.VMEM((2, width, rmax), BF16),
            pltpu.VMEM((2, width, rmax), BF16),
            pltpu.VMEM((2, 2 * rmax, rmax), BF16),
            pltpu.VMEM((2, 2 * rmax, rmax), BF16),
            pltpu.VMEM((2, width, rmax), BF16),
            pltpu.VMEM((2, width, rmax), BF16),
            pltpu.VMEM((2, rmax, rmax), BF16),
            pltpu.VMEM((2, rmax, rmax), F32),
            pltpu.VMEM((2, rmax, rmax), F32),
            pltpu.VMEM((rmax, rmax), BF16),
            pltpu.VMEM((2, rmax, 2 * rmax), F32),
            pltpu.SemaphoreType.DMA((32,)),
            pltpu.SemaphoreType.DMA((16,)),
        ],
        compiler_params=pltpu.CompilerParams(vmem_limit_bytes=56 * 1024 * 1024),
        cost_estimate=pl.CostEstimate(
            flops=16_000_000_000, bytes_accessed=20_000_000, transcendentals=0
        ),
    )(ranks, probe, upper, half, reach, gathered, *vparts, *uparts, trail_u, trail_v)


def on_device(
    trail_u,
    trail_v,
    tile_rank,
    new_rank,
    row_u,
    row_v,
    row_rank,
    col_u,
    col_v,
    col_rank,
    diag_inv,
    sketch,
):
    trow, _, width, rmax = trail_u.shape
    x, z = lax.axis_index("x"), lax.axis_index("z")
    yc = lax.axis_index(("y", "c"))
    pcol = z * 8 + yc
    trail_u, trail_v = trail_u[:, 0], trail_v[:, 0]

    gathered = lax.all_gather(pack(diag_inv, row_v, row_u), ("z", "y", "c"), axis=1, tiled=True)

    times = (0, 2, 3, 1)
    swap = [(a * 4 + q, (times[a] ^ q) * 4 + a) for a in range(4) for q in range(4)]
    quarter = lax.ppermute(jnp.stack([col_v, col_u], axis=1), ("x", "z"), swap)
    own_row = lax.dynamic_slice_in_dim(row_rank, x * trow, trow)
    own_col = lax.dynamic_slice_in_dim(col_rank, pcol, 1)
    turn = jnp.array(times, jnp.int32)[z]
    quarters = [(turn ^ lax.rem(x + 4 - k, 4))[None] for k in range(4)]
    ranks = jnp.concatenate([tile_rank[:, 0], new_rank[:, 0], own_row, own_col] + quarters)
    probe, upper, half = prepare(ranks, trail_u, trail_v, sketch)
    quarter, probe, upper, half = lax.optimization_barrier((quarter, probe, upper, half))
    quarter = lax.all_to_all(quarter, ("y", "c"), split_axis=0, concat_axis=2, tiled=True)[0]

    def spread(block):
        return [block] + [
            lax.ppermute(block, "x", [(a, (a + k) % 4) for a in range(4)]) for k in (1, 3, 2)
        ]

    vparts = spread(quarter[0])
    uparts = spread(quarter[1])
    vparts = [vparts[0], vparts[1], vparts[3], vparts[2]]
    uparts = [uparts[0], uparts[1], uparts[3], uparts[2]]

    reach = reach_of(ranks, sketch, uparts)
    fresh_u, fresh_v = tail(
        ranks, probe, upper, half, reach, gathered, vparts, uparts, trail_u, trail_v
    )
    return fresh_u[:, None], fresh_v[:, None]


def solution(mesh):
    split = Mesh(mesh.devices.reshape(4, 4, 4, 2), ("x", "z", "y", "c"))
    cols = ("z", "y", "c")
    tiles = P("x", cols, None, None)
    panel = P("x", cols, None)
    return jax.shard_map(
        on_device,
        mesh=split,
        in_specs=(
            tiles,
            tiles,
            P("x", cols),
            P("x", cols),
            panel,
            panel,
            P(),
            panel,
            panel,
            P(),
            P(cols, None),
            P(),
        ),
        out_specs=(tiles, tiles),
        check_vma=False,
    )
```

```python
import functools
import math

import jax
import jax.numpy as jnp
from jax import lax
from jax.experimental import pallas as pl
from jax.experimental.pallas import tpu as pltpu
from jax.sharding import Mesh, PartitionSpec as P

F32 = jnp.float32
BF16 = jnp.bfloat16
HALF = 128


def dot(a, b, ca=1, cb=0):
    return lax.dot_general(a, b, (((ca,), (cb,)), ((), ())), preferred_element_type=F32)


def pieces(x, count):
    out = []
    for _ in range(count):
        piece = x.astype(BF16)
        out.append(piece)
        x = x - piece.astype(F32)
    return out


def joined(a, b, pairs, ca=1, cb=0):
    left = jnp.concatenate([a[i] for i, _ in pairs], axis=ca)
    right = jnp.concatenate([b[j] for _, j in pairs], axis=cb)
    return dot(left, right, ca, cb)


ONE = ((0, 0), (1, 0), (2, 0))
SIX = ((0, 0), (0, 1), (1, 0), (1, 1), (0, 2), (2, 0))


def exact(a, b, ca=1, cb=0):
    return joined(pieces(a, 3), pieces(b, 3), SIX, ca, cb)


def tree(terms):
    while len(terms) > 1:
        terms = [a + b for a, b in zip(terms[::2], terms[1::2])] + (terms[-1:] if len(terms) % 2 else [])
    return terms[0]

def eliminate(blocks):
    n = HALF
    groups = n // 8
    lane = lax.broadcasted_iota(jnp.int32, (8, n), 1)
    sub = lax.broadcasted_iota(jnp.int32, (8, n), 0)
    spread = lambda v, r: jnp.broadcast_to(v[r : r + 1], (8, n))
    tiles = [[m[8 * i : 8 * i + 8] for i in range(groups)] for m in blocks]

    def column(v, at):
        return jnp.broadcast_to(jnp.sum(jnp.where(lane == at, v, 0.0), axis=1, keepdims=True), (8, n))

    for g in range(groups):
        panel = (lane >= 8 * g) & (lane < 8 * g + 8)
        for x in tiles:
            cols = [[column(x[i], 8 * g + j) for j in range(8)] for i in range(g, groups)]
            top, own, kept = x[g], list(cols[0]), x[g]
            raw, fresh = list(own), top
            for m in range(0, 8, 2):
                c0, c1 = own[m], own[m + 1]
                a, b, c = spread(raw[m], m), spread(raw[m + 1], m), spread(raw[m + 1], m + 1)
                inv = pl.reciprocal(a * c - b * b, approx=True)
                upper, lower = sub == m, sub == m + 1
                for j in range(m + 2, 8):
                    s0, s1 = spread(raw[j], m), spread(raw[j], m + 1)
                    h0, h1 = c * s0 - b * s1, a * s1 - b * s0
                    raw[j] = own[j] - inv * (c0 * h0 + c1 * h1)
                    own[j] = jnp.where(upper, inv * h0, jnp.where(lower, inv * h1, raw[j]))
                k = 8 * g + m
                first, second = lane == k, lane == k + 1
                if m:
                    kept = jnp.where(upper | lower, fresh, kept)
                r0, r1 = spread(fresh, m), spread(fresh, m + 1)
                r0 = jnp.where(first, 1.0, jnp.where(second, 0.0, r0))
                r1 = jnp.where(second, 1.0, jnp.where(first, 0.0, r1))
                h0, h1 = c * r0 - b * r1, a * r1 - b * r0
                fresh = jnp.where(first | second, 0.0, top) - inv * (c0 * h0 + c1 * h1)
                top = jnp.where(upper, inv * h0, jnp.where(lower, inv * h1, fresh))
            x[g] = kept
            if g + 1 < groups:
                solved = [spread(top, m) for m in range(8)]
                for t in range(1, groups - g):
                    terms = [cols[t][m] * solved[m] for m in range(8)]
                    x[g + t] = jnp.where(panel, 0.0, x[g + t]) - tree(terms)
    odd = (sub % 2) == 1
    out = []
    for x in tiles:
        done = []
        for i in range(groups):
            row = sub + 8 * i
            pivot_start = row - row % 2
            here = jnp.sum(jnp.where(lane == row, x[i], 0.0), axis=1, keepdims=True)
            above = jnp.sum(jnp.where((lane == row + 1) & ~odd, x[i], 0.0), axis=1, keepdims=True)
            here = jnp.broadcast_to(here, (8, n))
            above = jnp.broadcast_to(above, (8, n))
            unit = jnp.where(lane < pivot_start, x[i], jnp.where(lane == row, 1.0, 0.0))
            ratio = jnp.where(odd, pltpu.roll(above / here, 1, axis=0), 0.0)
            above = jnp.where(odd, pltpu.roll(above, 1, axis=0), 0.0)
            scale = lax.rsqrt(here - ratio * above)
            done.append((unit - ratio * pltpu.roll(unit, 1, axis=0)) * scale)
        out.append(jnp.concatenate(done, axis=0))
    return out


def inverse_factors(grams):
    h = HALF
    n = 2 * h
    diagonal = lax.broadcasted_iota(jnp.int32, (n, n), 0) == lax.broadcasted_iota(
        jnp.int32, (n, n), 1
    )
    scales, scaled = [], []
    for g in grams:
        kept = jnp.where(diagonal, g, 0.0)
        across = lax.rsqrt(jnp.sum(kept, axis=0, keepdims=True))
        down = lax.rsqrt(jnp.sum(kept, axis=1, keepdims=True))
        scales.append(across)
        scaled.append((g * down) * across)
    m1 = eliminate([g[:h, :h] for g in scaled])
    u12 = [exact(m, g[:h, h:]) for m, g in zip(m1, scaled)]
    m2 = eliminate([g[h:, h:] - exact(u, u, 0, 0) for u, g in zip(u12, scaled)])
    m21 = [-exact(b, exact(u, a, 0, 0)) for a, b, u in zip(m1, m2, u12)]
    zero = jnp.zeros((h, h), F32)
    return [
        jnp.concatenate(
            [jnp.concatenate([a, zero], axis=1), jnp.concatenate([c, b], axis=1)], axis=0
        )
        * scale
        for a, b, c, scale in zip(m1, m2, m21, scales)
    ]


def pack_kernel(diag, row_v, row_u, out, wide, narrow, sem):
    chunks, _, rmax = narrow.shape
    copies = [
        pltpu.make_async_copy(row_v, out.at[pl.ds(chunks, 2)], sem.at[0]),
        pltpu.make_async_copy(row_u, out.at[pl.ds(chunks + 2, 2)], sem.at[1]),
    ]
    loads = []
    for k in range(4):
        columns = pl.ds(2 * rmax * k, 2 * rmax)
        loads.append(
            pltpu.make_async_copy(diag.at[:, columns], wide.at[:, columns], sem.at[2 + k])
        )
    for copy in loads + copies:
        copy.start()
    for k in range(4):
        loads[k].wait()
        for c in (2 * k, 2 * k + 1):
            narrow[c] = wide[:, rmax * c : rmax * (c + 1)].astype(BF16)
        pair = pl.ds(2 * k, 2)
        copies.append(pltpu.make_async_copy(narrow.at[pair], out.at[pair], sem.at[6 + k]))
        copies[-1].start()
    for copy in copies:
        copy.wait()


def pack(diag_inv, row_v, row_u):
    count, slab, rmax = row_v.shape
    chunks = diag_inv.shape[1] // rmax
    hbm = pl.BlockSpec(memory_space=pl.ANY)
    return pl.pallas_call(
        pack_kernel,
        name="pack",
        out_shape=jax.ShapeDtypeStruct((chunks + 2 * count, slab, rmax), BF16),
        in_specs=[hbm] * 3,
        out_specs=hbm,
        scratch_shapes=[
            pltpu.VMEM(diag_inv.shape, F32),
            pltpu.VMEM((chunks, slab, rmax), BF16),
            pltpu.SemaphoreType.DMA((10,)),
        ],
        cost_estimate=pl.CostEstimate(flops=0, bytes_accessed=1_100_000, transcendentals=0),
    )(diag_inv, row_v, row_u)


def prepare_kernel(ranks, tu, tv, sk, probe, upper, gram):
    rmax = sk.shape[1]
    t = pl.program_id(0)
    row = lax.broadcasted_iota(jnp.int32, (rmax, rmax), 0)
    col = lax.broadcasted_iota(jnp.int32, (rmax, rmax), 1)
    p = dot(tv[0], sk[...], 0, 0)
    p = jnp.where((row < ranks[t]) & (col < ranks[2 + t]), p, 0.0).astype(BF16)
    h = sum(dot(piece, p) for piece in pieces(dot(tu[0], tu[0], 0, 0), 3))
    probe[0] = p
    upper[0] = h
    gram[0] = 0.5 * sum(dot(p, piece, 0, 0) for piece in pieces(h, 3))


def prepare(ranks, trail_u, trail_v, sketch):
    width, rmax = sketch.shape
    square = lambda kind: jax.ShapeDtypeStruct((2, rmax, rmax), kind)
    tile = pl.BlockSpec((1, width, rmax), lambda t: (t, 0, 0))
    small = pl.BlockSpec((1, rmax, rmax), lambda t: (t, 0, 0))
    return pl.pallas_call(
        prepare_kernel,
        name="prepare",
        grid=(2,),
        out_shape=(square(BF16), square(F32), square(F32)),
        in_specs=[
            pl.BlockSpec(memory_space=pltpu.SMEM),
            tile,
            tile,
            pl.BlockSpec((width, rmax), lambda t: (0, 0)),
        ],
        out_specs=(small, small, small),
        compiler_params=pltpu.CompilerParams(vmem_limit_bytes=24 * 1024 * 1024),
        cost_estimate=pl.CostEstimate(
            flops=2_000_000_000, bytes_accessed=6_000_000, transcendentals=0
        ),
    )(ranks, trail_u, trail_v, sketch)


def reach_kernel(ranks, sk, up0, up1, up2, up3, out):
    part = up0.shape[0]
    total = None
    for k, block in enumerate((up0, up1, up2, up3)):
        at = pl.multiple_of(ranks[7 + k] * part, part)
        term = dot(block[...], sk[pl.ds(at, part)], 0, 0)
        total = term if total is None else total + term
    out[...] = total.astype(BF16)


def reach_of(ranks, sketch, uparts):
    rmax = sketch.shape[1]
    vmem = pl.BlockSpec(memory_space=pltpu.VMEM)
    return pl.pallas_call(
        reach_kernel,
        name="reach",
        out_shape=jax.ShapeDtypeStruct((rmax, rmax), BF16),
        in_specs=[pl.BlockSpec(memory_space=pltpu.SMEM)] + [vmem] * 5,
        out_specs=vmem,
        compiler_params=pltpu.CompilerParams(vmem_limit_bytes=12 * 1024 * 1024),
        cost_estimate=pl.CostEstimate(
            flops=300_000_000, bytes_accessed=2_200_000, transcendentals=0
        ),
    )(ranks, sketch, *uparts)


def tail_kernel(
    ranks,
    probe,
    upper,
    half,
    reach,
    gathered,
    vp0,
    vp1,
    vp2,
    vp3,
    up0,
    up1,
    up2,
    up3,
    trail_u,
    trail_v,
    fresh_u,
    fresh_v,
    dinv,
    vall,
    wall,
    ui,
    uj,
    tu,
    tv,
    zs,
    bs,
    ou,
    ov,
    pv,
    hv,
    gv,
    rv,
    ps,
    load_sem,
    out_sem,
):
    width, rmax = uj.shape
    part = width // 4
    smalls = (pv, hv, gv, rv)
    loads = []

    def load(src, dst):
        copy = pltpu.make_async_copy(src, dst, load_sem.at[len(loads)])
        copy.start()
        loads.append(copy)
        return copy

    def spots():
        return [pl.multiple_of(ranks[7 + k] * part, part) for k in range(4)]

    def load_d(q):
        chunks, rows = pl.ds(0, 2 * q + 2), pl.ds(part * q, part)
        return load(gathered.at[chunks, rows], dinv.at[chunks, rows])

    def load_quarter(q):
        rows = pl.ds(part * q, part)
        copies = [
            load(gathered.at[8 + t, rows], vall.at[rows, pl.ds(rmax * t, rmax)]) for t in range(2)
        ]
        for n in range(2):
            chunks, block = pl.ds(0, 2 * q + 1 + n), pl.ds(part * q + rmax * n, rmax)
            copies.append(load(gathered.at[chunks, block], dinv.at[chunks, block]))
        return copies

    need_vj = [
        load(a, vall.at[pl.ds(at, part), pl.ds(2 * rmax, rmax)])
        for at, a in zip(spots(), (vp0, vp1, vp2, vp3))
    ]
    need = [load_quarter(0), load_quarter(1)]
    need_u = [load(gathered.at[10 + t], ui.at[t]) for t in range(2)]
    need_u.append(load(trail_u, tu))
    need += [load_quarter(2), load_quarter(3)]
    for copy in need_vj:
        copy.wait()
    for q in range(4):
        for copy in need[q]:
            copy.wait()
        if q == 1:
            need_smalls = [load(a, b) for a, b in zip((probe, upper, half, reach), smalls)]
        if q == 2:
            rest = [load(a, uj.at[pl.ds(at, part)]) for at, a in zip(spots(), (up0, up1, up2, up3))]
            rest.append(load(trail_v, tv))
        for n in range(2):
            at = part * q + rmax * n
            count = 2 * q + 1 + n
            lhs = jnp.concatenate([dinv[c, at : at + rmax] for c in range(count)], axis=1)
            wall[at : at + rmax] = dot(lhs, vall[: rmax * count]).astype(BF16)
        if q == 1:
            for copy in need_u:
                copy.wait()
            for t in range(2):
                sides = jnp.concatenate([tu[t], ui[t]], axis=1)
                ps[t] = dot(ui[t], sides, 0, 0)
    for copy in need_smalls:
        copy.wait()
    probe, upper, half, reach = smalls
    parts = [(pieces(ps[t, :, :rmax], 3), pieces(ps[t, :, rmax:], 3)) for t in range(2)]
    crosses = [joined(parts[t][0], [probe[t]], ONE) for t in range(2)]
    coupling = dot(wall[:, : 2 * rmax], wall[:, 2 * rmax :], 0, 0)

    row = lax.broadcasted_iota(jnp.int32, (rmax, rmax), 0)
    col = lax.broadcasted_iota(jnp.int32, (rmax, rmax), 1)
    couplings, grams, probes, products = [], [], [], []
    for t in range(2):
        new_rank, row_rank, col_rank = ranks[2 + t], ranks[4 + t], ranks[6]
        keep = col < new_rank
        top = probe[t]
        c = coupling[rmax * t : rmax * (t + 1)]
        c = jnp.where((row < row_rank) & (col < col_rank), c, 0.0).astype(BF16)
        bottom = jnp.where(keep, -dot(c, reach[...]), 0.0).astype(BF16)
        gru, grr = parts[t]
        cross = crosses[t]
        own = joined(grr, [bottom], ONE)
        mixed = pieces(cross + 0.5 * own, 3)
        gram = half[t] + joined([bottom], mixed, ((0, 0), (0, 1), (0, 2)), 0, 0)
        grams.append(gram + gram.T + jnp.where((row == col) & ~keep, 1.0, 0.0))
        couplings.append(c)
        probes.append(jnp.concatenate([top, bottom], axis=0))
        above = upper[t] + joined(gru, [bottom], ONE[:2], 0, 0)
        products.append(pieces(jnp.concatenate([above, cross + own], axis=0), 2))
    inverses = inverse_factors(grams)
    for t in range(2):
        m = pieces(inverses[t] * math.sqrt(width), 2)
        zs[t] = joined([probes[t]], m, ((0, 0), (0, 1)), 1, 1).astype(BF16)
        back = joined(products[t], m, ((0, 0), (0, 1), (1, 0)), 1, 1)
        top = jnp.where(row < ranks[t], back[:rmax], 0.0)
        bottom = -dot(couplings[t], back[rmax:].astype(BF16), 0, 0)
        bs[t] = (jnp.concatenate([top, bottom], axis=0) / width).astype(BF16)
    for copy in rest:
        copy.wait()

    copies = []
    for t in range(2):
        for n in range(4):
            rows = pl.ds(part * n, part)
            left = jnp.concatenate([tu[t, rows], ui[t, rows]], axis=1)
            ou[t, rows] = dot(left, zs[t]).astype(BF16)
            right = jnp.concatenate([tv[t, rows], uj[rows]], axis=1)
            ov[t, rows] = dot(right, bs[t]).astype(BF16)
            for src, dst in ((ou, fresh_u), (ov, fresh_v)):
                copy = pltpu.make_async_copy(
                    src.at[t, rows], dst.at[t, rows], out_sem.at[len(copies)]
                )
                copy.start()
                copies.append(copy)
    for copy in copies:
        copy.wait()


def tail(ranks, probe, upper, half, reach, gathered, vparts, uparts, trail_u, trail_v):
    _, width, rmax = trail_u.shape
    hbm = pl.BlockSpec(memory_space=pl.ANY)
    tile = jax.ShapeDtypeStruct(trail_u.shape, BF16)
    return pl.pallas_call(
        tail_kernel,
        name="tail",
        out_shape=(tile, tile),
        in_specs=[pl.BlockSpec(memory_space=pltpu.SMEM)] + [hbm] * 15,
        out_specs=(hbm, hbm),
        scratch_shapes=[
            pltpu.VMEM((8, width, rmax), BF16),
            pltpu.VMEM((width, 3 * rmax), BF16),
            pltpu.VMEM((width, 3 * rmax), BF16),
            pltpu.VMEM((2, width, rmax), BF16),
            pltpu.VMEM((width, rmax), BF16),
            pltpu.VMEM((2, width, rmax), BF16),
            pltpu.VMEM((2, width, rmax), BF16),
            pltpu.VMEM((2, 2 * rmax, rmax), BF16),
            pltpu.VMEM((2, 2 * rmax, rmax), BF16),
            pltpu.VMEM((2, width, rmax), BF16),
            pltpu.VMEM((2, width, rmax), BF16),
            pltpu.VMEM((2, rmax, rmax), BF16),
            pltpu.VMEM((2, rmax, rmax), F32),
            pltpu.VMEM((2, rmax, rmax), F32),
            pltpu.VMEM((rmax, rmax), BF16),
            pltpu.VMEM((2, rmax, 2 * rmax), F32),
            pltpu.SemaphoreType.DMA((32,)),
            pltpu.SemaphoreType.DMA((16,)),
        ],
        compiler_params=pltpu.CompilerParams(vmem_limit_bytes=56 * 1024 * 1024),
        cost_estimate=pl.CostEstimate(
            flops=16_000_000_000, bytes_accessed=20_000_000, transcendentals=0
        ),
    )(ranks, probe, upper, half, reach, gathered, *vparts, *uparts, trail_u, trail_v)


def on_device(
    trail_u,
    trail_v,
    tile_rank,
    new_rank,
    row_u,
    row_v,
    row_rank,
    col_u,
    col_v,
    col_rank,
    diag_inv,
    sketch,
):
    trow, _, width, rmax = trail_u.shape
    x, z = lax.axis_index("x"), lax.axis_index("z")
    yc = lax.axis_index(("y", "c"))
    pcol = z * 8 + yc
    trail_u, trail_v = trail_u[:, 0], trail_v[:, 0]

    gathered = lax.all_gather(pack(diag_inv, row_v, row_u), ("z", "y", "c"), axis=1, tiled=True)

    times = (0, 2, 3, 1)
    swap = [(a * 4 + q, (times[a] ^ q) * 4 + a) for a in range(4) for q in range(4)]
    quarter = lax.ppermute(jnp.stack([col_v, col_u], axis=1), ("x", "z"), swap)
    own_row = lax.dynamic_slice_in_dim(row_rank, x * trow, trow)
    own_col = lax.dynamic_slice_in_dim(col_rank, pcol, 1)
    turn = jnp.array(times, jnp.int32)[z]
    quarters = [(turn ^ lax.rem(x + 4 - k, 4))[None] for k in range(4)]
    ranks = jnp.concatenate([tile_rank[:, 0], new_rank[:, 0], own_row, own_col] + quarters)
    probe, upper, half = prepare(ranks, trail_u, trail_v, sketch)
    quarter, probe, upper, half = lax.optimization_barrier((quarter, probe, upper, half))
    quarter = lax.all_to_all(quarter, ("y", "c"), split_axis=0, concat_axis=2, tiled=True)[0]

    def spread(block):
        return [block] + [
            lax.ppermute(block, "x", [(a, (a + k) % 4) for a in range(4)]) for k in (1, 3, 2)
        ]

    vparts = spread(quarter[0])
    uparts = spread(quarter[1])
    vparts = [vparts[0], vparts[1], vparts[3], vparts[2]]
    uparts = [uparts[0], uparts[1], uparts[3], uparts[2]]

    reach = reach_of(ranks, sketch, uparts)
    fresh_u, fresh_v = tail(
        ranks, probe, upper, half, reach, gathered, vparts, uparts, trail_u, trail_v
    )
    return fresh_u[:, None], fresh_v[:, None]


def solution(mesh):
    split = Mesh(mesh.devices.reshape(4, 4, 4, 2), ("x", "z", "y", "c"))
    cols = ("z", "y", "c")
    tiles = P("x", cols, None, None)
    panel = P("x", cols, None)
    return jax.shard_map(
        on_device,
        mesh=split,
        in_specs=(
            tiles,
            tiles,
            P("x", cols),
            P("x", cols),
            panel,
            panel,
            P(),
            panel,
            panel,
            P(),
            P(cols, None),
            P(),
        ),
        out_specs=(tiles, tiles),
        check_vma=False,
    )
```
